32 devices in a mesh: wide: 8 (over y, x, core), narrow: 4 (over z).
Axes of the slice: x: 2, y: 2, z: 4, core: 2. Of those that a mesh axis runs over, the one named last changes fastest.
Arguments:
- points: float32 [8, 16384], P(None, 'narrow'), may hold values from 0 to 1
- scales: float32 [8], replicated, may hold values from 2 to 6
- frequencies: float32 [8, 32768], P(None, 'wide'), may hold values from -24 to 24
- phases: float32 [32768], P('wide'), may hold values from -3.140625 to 3.140625
- feature_weights: bfloat16 [64, 32768], P(None, 'wide'), may hold values from -6 to 6
- targets: float32 [16384], P(('narrow', 'wide')), may hold values from -6 to 6
- noise: float32 [64, 16384], P(None, ('narrow', 'wide')), may hold values from -1.8 to 1.8
- inverses: float32 [2, 8192, 8192], P(None, 'wide', 'narrow'), may hold values from -0.01767767 to 1.0176777
- groups: int32 [2, 64], replicated, may hold values from 0 to 127, as said below
Outputs:
- residual: float32 [64, 16384], P(None, ('narrow', 'wide'))
- weights: float32 [2, 64, 8192], P(None, None, 'wide')
The draws below stay inside these ranges and needn't reach their ends.
Inputs may be any that keep to these rules, and one draw needn't show every extreme that they name: All entries differ; each names the group of points g * 128 to g * 128 + 127. In every block, the entries n * 16 to (n + 1) * 16 - 1 name groups of narrow index n's points, that is groups n * 32 to (n + 1) * 32 - 1.
All inputs are finite; a program needn't handle non-finite values.
Results may differ from the reference program's by a relative error of at most 0.00065.
Values may be sent and summed in bfloat16 or wider, within the bound.
No kernel may reach another device: no remote copies, remote signals or barrier semaphores. Data moves between devices by JAX's collectives and lax.ppermute only.
A program may use at most 128 MiB of HBM per device.

```python
import math
import jax
import jax.numpy as jnp
from jax import lax

D = 8
FEATURES = 32768
SAMPLES = 64
BLOCK = 8192
GROUP = 128
BLOCKS = 2
SHARD_PTS = 4096
POINTS = 16384
N_NARROW = 4


def draw_inverses(key, part):
    first_key, second_key = jax.random.split(jax.random.fold_in(key, 11))
    diagonal = jax.random.uniform(first_key, (BLOCKS, BLOCK), jnp.float32, 0.5, 1.0)
    offdiag = jax.random.truncated_normal(second_key, -4.0, 4.0, (BLOCKS, BLOCK, BLOCK), jnp.float32) * (0.4 / math.sqrt(BLOCK))
    positions = jnp.arange(BLOCK)
    return offdiag.at[:, positions, positions].add(diagonal)


def draw_groups(key, part):
    per_shard = SHARD_PTS // GROUP
    taken = BLOCK // (N_NARROW * GROUP)
    shard_keys = jax.random.split(jax.random.fold_in(key, 23), N_NARROW)
    orders = jax.vmap(lambda one_key: jax.random.permutation(one_key, per_shard))(shard_keys)
    chosen = orders[:, :BLOCKS * taken].astype(jnp.int32) + (jnp.arange(N_NARROW, dtype=jnp.int32) * per_shard)[:, None]
    chosen = chosen.reshape(N_NARROW, BLOCKS, taken)
    return jnp.transpose(chosen, (1, 0, 2)).reshape(BLOCKS, N_NARROW * taken).astype(jnp.int32)


def block_levels(key, extent, shards, smallest, high):
    def one(axis_at, blocks):
        draws = jax.random.uniform(jax.random.fold_in(jax.random.fold_in(key, 6), axis_at), (blocks,), jnp.float32, smallest / len(shards), high / len(shards))
        return jnp.repeat(jnp.exp(draws), extent[axis_at] // blocks).reshape((-1,) + (1,) * (len(extent) - axis_at - 1))

    level = one(*shards[0])
    for cut in shards[1:]:
        level = level * one(*cut)
    return level


def gaussian(rng, shape, scale, limit, cuts=(), kind=jnp.bfloat16):
    entries = scale * jax.random.normal(rng, shape, jnp.float32)
    if cuts:
        entries = entries * block_levels(rng, shape, cuts, -0.22, 0.18)
    return jnp.clip(entries, -limit, limit).astype(kind)


def setup_inputs(seed: int = 0) -> dict:
    key_list = jax.random.split(jax.random.key(seed), 10)
    points = jnp.clip(1.0 * jax.random.uniform(key_list[0], (D, POINTS), jnp.float32) ** block_levels(key_list[0], (D, POINTS), ((1, 4),), -0.2, 0.2), 0.0, 1.0)
    scales = jnp.clip(jnp.exp(jax.random.uniform(key_list[1], (D,), jnp.float32, math.log(2.0), math.log(6.0))), 2.0, 6.0)
    frequencies = gaussian(key_list[2], (D, FEATURES), 4.0, 24.0, ((1, 8),), jnp.float32)
    phases = jnp.clip(jax.random.uniform(key_list[3], (FEATURES,), jnp.float32, -3.140625, 3.140625), -3.140625, 3.140625)
    feature_weights = gaussian(key_list[4], (SAMPLES, FEATURES), 1.0, 6.0, ((1, 8),))
    targets = gaussian(key_list[5], (POINTS,), 1.0, 6.0, ((0, 32),), jnp.float32)
    noise = gaussian(key_list[6], (SAMPLES, POINTS), 0.3, 1.8, ((1, 32),), jnp.float32)
    inverses = draw_inverses(jax.random.fold_in(key_list[9], 71), 0)
    groups = draw_groups(jax.random.fold_in(key_list[9], 71), 0)
    return dict(points=points, scales=scales, frequencies=frequencies, phases=phases, feature_weights=feature_weights, targets=targets, noise=noise, inverses=inverses, groups=groups)


NOISE_VAR = 0.1
ROOT_FIVE = math.sqrt(5.0)
HIGH = lax.Precision.HIGHEST

def matern_tile(rows_coords, cols_coords, row_ids, col_ids):
    dist_sq = jnp.zeros((rows_coords.shape[1], cols_coords.shape[1]), rows_coords.dtype)
    for coord in range(rows_coords.shape[0]):
        differ = rows_coords[coord][:, None] - cols_coords[coord][None, :]
        dist_sq = dist_sq + differ * differ
    scaled = ROOT_FIVE * jnp.sqrt(dist_sq)
    values = (1.0 + scaled + scaled * scaled / 3.0) * jnp.exp(-scaled)
    return values + jnp.where(row_ids[:, None] == col_ids[None, :], NOISE_VAR, 0.0)

def reference(points, scales, frequencies, phases, feature_weights, targets, noise, inverses, groups):
    total_points = points.shape[1]
    pblock = math.gcd(total_points, 512)

    def prior_block(index):
        coords = lax.dynamic_slice_in_dim(points, index * pblock, pblock, 1)
        angles = jnp.dot(frequencies.T, coords, precision=HIGH, preferred_element_type=jnp.float32) + phases[:, None]
        features = jnp.cos(angles).astype(jnp.bfloat16)
        return jnp.dot(feature_weights, features, preferred_element_type=jnp.float32)
    blocks = lax.map(prior_block, jnp.arange(total_points // pblock, dtype=jnp.int32))
    prior = jnp.transpose(blocks, (1, 0, 2)).reshape(SAMPLES, total_points)
    residual = targets[None, :] - math.sqrt(2.0 / FEATURES) * prior - noise
    scaled = scales[:, None] * points
    col_ids_all = jnp.arange(total_points, dtype=jnp.int32)
    cblock = math.gcd(total_points, 2048)
    weight_list = []
    for block_index in range(BLOCKS):
        member_ids = (groups[block_index][:, None] * GROUP + jnp.arange(GROUP, dtype=jnp.int32)[None, :]).reshape(-1)
        picked = jnp.take(residual, member_ids, axis=1)
        update = jnp.dot(picked, inverses[block_index].T, precision=HIGH, preferred_element_type=jnp.float32)
        row_coords = jnp.take(scaled, member_ids, axis=1)

        def kernel_block(index):
            begin = index * cblock
            tile = matern_tile(row_coords, lax.dynamic_slice_in_dim(scaled, begin, cblock, 1), member_ids, lax.dynamic_slice_in_dim(col_ids_all, begin, cblock, 0))
            return jnp.dot(update, tile, precision=HIGH, preferred_element_type=jnp.float32)
        parts = lax.map(kernel_block, jnp.arange(total_points // cblock, dtype=jnp.int32))
        residual = residual - jnp.transpose(parts, (1, 0, 2)).reshape(SAMPLES, total_points)
        weight_list.append(update)
    return (residual, jnp.stack(weight_list))
```

```python
import functools
import math

import jax
import jax.numpy as jnp
from jax import lax
from jax.experimental import pallas as pl
from jax.experimental.pallas import tpu as pltpu
from jax.sharding import PartitionSpec as P

GROUP = 128
BLOCKS = 2
NOISE_VAR = 0.1
LN2 = math.log(2.0)
TO_TURNS = 1.0 / (2.0 * math.pi)
TO_U = math.sqrt(5.0) / LN2
SINE = (-6.283164044164058, 41.33714235333657, -81.34076831835199, 70.99342806157215)
VMEM = 44 << 20
F32 = jnp.float32
BF16 = jnp.bfloat16


def thirds(x):
    high = x.astype(BF16).astype(F32)
    rest = x - high
    mid = rest.astype(BF16).astype(F32)
    low = (rest - mid).astype(BF16).astype(F32)
    return high, mid, low


def halves(x):
    high = x.astype(BF16)
    return high, (x - high.astype(F32)).astype(BF16)


def stack_rows(rows):
    width = max(row.shape[1] for row in rows)
    at = lax.broadcasted_iota(jnp.int32, (8, width), 0)
    out = jnp.zeros((8, width), F32)
    for index, row in enumerate(rows):
        out = jnp.where(at == index, row, out)
    return out


def left_terms(parts, extra):
    high, mid, low = parts
    return jnp.concatenate([high, high, mid, mid, high, low, extra, jnp.zeros_like(high)], 0)


def right_terms(parts, extra):
    high, mid, low = parts
    return jnp.concatenate([high, mid, high, mid, low, high, extra, jnp.zeros_like(high)], 0)


def cosine(turns):
    fraction = turns - jnp.round(turns)
    shifted = jnp.abs(fraction) - 0.25
    square = shifted * shifted
    value = SINE[-1]
    for factor in SINE[-2::-1]:
        value = value * square + factor
    return value * shifted


def group_of(ref, index):
    return ref[:, pl.ds(pl.multiple_of(index * GROUP, GROUP), GROUP)]


def whole_block(array):
    return pl.BlockSpec(array.shape, lambda i, *_: (0,) * array.ndim)


def prior_body(
    tile, chunk, own, factor, order, place, freq, phase, fw, points, targets, noise, out, left
):
    features = freq.shape[1]

    @pl.when(pl.program_id(0) == 0)
    def _():
        step = math.gcd(features, 512)
        for begin in range(0, features, step):
            cut = slice(begin, begin + step)
            extra = stack_rows(thirds(phase[:, cut] * TO_TURNS))
            terms = left_terms(thirds(freq[:, cut] * TO_TURNS), extra)
            left[cut, :] = terms.T.astype(BF16)

    per = tile // GROUP
    first = pl.program_id(0) * per
    coords = jnp.concatenate([group_of(points, order[first + k]) for k in range(per)], 1)
    ones = jnp.ones((1, tile), F32)
    right = right_terms(thirds(coords), stack_rows([ones] * 3)).astype(BF16)
    total = jnp.zeros(out.shape, F32)
    for begin in range(0, features, chunk):
        turns = jnp.dot(left[begin : begin + chunk, :], right, preferred_element_type=F32)
        values = cosine(turns).astype(BF16)
        total += jnp.dot(fw[:, begin : begin + chunk], values, preferred_element_type=F32)
    out[...] = -factor * total
    for k in range(per):
        group = order[first + k]

        @pl.when(group // own == place[0])
        def _():
            inside = lax.rem(group, own)
            cut = slice(k * GROUP, (k + 1) * GROUP)
            out[:, cut] += group_of(targets, inside) - group_of(noise, inside)


def prior_part(order, place, own, factor, freq, phase, fw, points, targets, noise, name):
    samples, features = fw.shape
    width = order.shape[0] * GROUP
    tile = math.gcd(width, 512)
    body = functools.partial(prior_body, tile, math.gcd(features, 2048), own, factor)
    arrays = (freq, phase, fw, points, targets, noise)
    return pl.pallas_call(
        body,
        out_shape=jax.ShapeDtypeStruct((samples, width), F32),
        grid_spec=pltpu.PrefetchScalarGridSpec(
            num_scalar_prefetch=2,
            grid=(width // tile,),
            in_specs=[whole_block(array) for array in arrays],
            out_specs=pl.BlockSpec((samples, tile), lambda i, *_: (0, i)),
            scratch_shapes=[pltpu.VMEM((features, 64), BF16)],
        ),
        compiler_params=pltpu.CompilerParams(vmem_limit_bytes=VMEM),
        cost_estimate=pl.CostEstimate(
            flops=14 * features * width + 2 * (samples + 64) * features * width,
            bytes_accessed=samples * (2 * features + 4 * width),
            transcendentals=features * width,
        ),
        name=name,
    )(order, place, *arrays)


def inverse_body(x, inverse, out, terms):
    samples = x.shape[0]

    @pl.when(pl.program_id(0) == 0)
    def _():
        high, low = halves(x[...])
        terms[:samples, :] = high
        terms[samples:, :] = low

    high, low = halves(inverse[...])
    dims = (((1,), (1,)), ((), ()))
    both = lax.dot_general(terms[...], high, dims, preferred_element_type=F32)
    rest = lax.dot_general(terms[:samples, :], low, dims, preferred_element_type=F32)
    out[...] = both[:samples] + both[samples:] + rest


def inverse_part(x, inverses, block, name):
    samples, depth = x.shape
    rows = inverses.shape[1]
    tile = math.gcd(rows, 256)
    return pl.pallas_call(
        inverse_body,
        out_shape=jax.ShapeDtypeStruct((samples, rows), F32),
        grid=(rows // tile,),
        in_specs=[
            whole_block(x),
            pl.BlockSpec((None, tile, depth), lambda i: (block, i, 0)),
        ],
        out_specs=pl.BlockSpec((samples, tile), lambda i: (0, i)),
        scratch_shapes=[pltpu.VMEM((2 * samples, depth), BF16)],
        compiler_params=pltpu.CompilerParams(vmem_limit_bytes=VMEM),
        cost_estimate=pl.CostEstimate(
            flops=6 * samples * rows * depth, bytes_accessed=4 * rows * depth, transcendentals=0
        ),
        name=name,
    )(x, inverses)


def kernel_coords(coords, scales):
    centred = (coords - 0.5) * (scales * TO_U)
    return centred, jnp.sum(centred * centred, axis=0, keepdims=True)


def kernel_body(
    tile, start, block, own, shuffle, order, rows, place, every, scales, update, carry, out, left, terms
):
    samples = update.shape[0]
    groups = rows.shape[0]

    @pl.when(pl.program_id(0) == 0)
    def _():
        for j in range(groups):
            group = rows[j]
            owner, inside = group // place[3], lax.rem(group, place[3])
            coords = every[owner, :, pl.ds(pl.multiple_of(inside * GROUP, GROUP), GROUP)]
            centred, norm = kernel_coords(coords, scales[...])
            ones = jnp.ones((1, GROUP), F32)
            extra = stack_rows([*thirds(norm), ones, ones, ones])
            matrix = left_terms([-2.0 * part for part in thirds(centred)], extra)
            left[j * GROUP : (j + 1) * GROUP, :] = matrix.T.astype(BF16)
        high, low = halves(update[...])
        terms[:samples, :] = high
        terms[samples:, :] = low

    per = tile // GROUP
    first = pl.program_id(0) * per
    coords = jnp.concatenate(
        [
            every[place[1], :, pl.ds(pl.multiple_of(order[first + k] * GROUP, GROUP), GROUP)]
            for k in range(per)
        ],
        1,
    )
    centred, norm = kernel_coords(coords, scales[...])
    ones = jnp.ones((1, tile), F32)
    right = right_terms(thirds(centred), stack_rows([ones, ones, ones, *thirds(norm)])).astype(BF16)
    square = jnp.dot(left[...], right, preferred_element_type=F32)
    square = jnp.maximum(square, 1e-20)
    u = square * lax.rsqrt(square)
    values = (1.0 + u * (LN2 + (LN2 * LN2 / 3.0) * u)) * jnp.exp2(-u)
    high, low = halves(values)
    both = jnp.dot(terms[...], high, preferred_element_type=F32)
    rest = jnp.dot(terms[:samples, :], low, preferred_element_type=F32)
    total = both[:samples] + both[samples:] + rest
    for k in range(per):
        entry = first + k + start - block * place[2]
        row = place[1] * place[2] + entry - place[0] * groups
        mine = (entry >= 0) & (entry < place[2]) & (row >= 0) & (row < groups)
        weight = jnp.where(mine, NOISE_VAR, 0.0)
        cut = slice(k * GROUP, (k + 1) * GROUP)
        diagonal = group_of(update, jnp.clip(row, 0, groups - 1))
        value = carry[:, cut] - total[:, cut] - weight * diagonal
        if shuffle:
            group = order[first + k]
            inside = pl.multiple_of(lax.rem(group, own) * GROUP, GROUP)
            out[group // own, :, pl.ds(inside, GROUP)] = value
        else:
            out[:, cut] = value


def kernel_part(order, rows, place, every, scales, update, carry, start, block, own, shuffle, name):
    samples = update.shape[0]
    width = order.shape[0] * GROUP
    tile = math.gcd(width, 256)
    parts = width // (own * GROUP)
    shape = (parts, samples, own * GROUP) if shuffle else (samples, width)
    if shuffle:
        out_spec = pl.BlockSpec(shape, lambda i, *_: (0, 0, 0))
    else:
        out_spec = pl.BlockSpec((samples, tile), lambda i, *_: (0, i))
    depth = rows.shape[0] * GROUP
    return pl.pallas_call(
        functools.partial(kernel_body, tile, start, block, own, shuffle),
        out_shape=jax.ShapeDtypeStruct(shape, F32),
        grid_spec=pltpu.PrefetchScalarGridSpec(
            num_scalar_prefetch=3,
            grid=(width // tile,),
            in_specs=[
                whole_block(every),
                whole_block(scales),
                whole_block(update),
                pl.BlockSpec((samples, tile), lambda i, *_: (0, i)),
            ],
            out_specs=out_spec,
            scratch_shapes=[
                pltpu.VMEM((depth, 64), BF16),
                pltpu.VMEM((2 * samples, depth), BF16),
            ],
        ),
        compiler_params=pltpu.CompilerParams(vmem_limit_bytes=VMEM),
        cost_estimate=pl.CostEstimate(
            flops=14 * depth * width + 6 * (samples + 20) * depth * width,
            bytes_accessed=8 * samples * width,
            transcendentals=2 * depth * width,
        ),
        name=name,
    )(order, rows, place, every, scales, update, carry)


def exchange(value, axis, mask):
    count = lax.axis_size(axis)
    return lax.ppermute(value, axis, [(i, i ^ mask) for i in range(count)])


def butterfly(value, axis, masks):
    if not masks:
        return value
    if len(masks) == 1:
        return value + exchange(value, axis, masks[0])
    rows = value.shape[0] // 2
    upper, lower = value[:rows], value[rows:]
    turned = masks[1:] + masks[:1]
    for one, two in zip(masks, turned):
        got_upper, got_lower = exchange(upper, axis, one), exchange(lower, axis, two)
        upper, lower = upper + got_upper, lower + got_lower
    return jnp.concatenate([upper, lower], 0)


def sum_wide(value):
    count = lax.axis_size("wide")
    if count & (count - 1) or count < 2:
        return lax.psum(value, "wide")
    core = lax.rem(lax.axis_index("wide"), 2)
    rows = value.shape[0] // 2
    mine = lax.dynamic_slice_in_dim(value, core * rows, rows, 0)
    other = lax.dynamic_slice_in_dim(value, (1 - core) * rows, rows, 0)
    summed = mine + exchange(other, "wide", 1)
    summed = butterfly(summed, "wide", [1 << bit for bit in range(1, count.bit_length() - 1)])
    got = exchange(summed, "wide", 1)
    first = core == 0
    return jnp.concatenate([jnp.where(first, summed, got), jnp.where(first, got, summed)], 0)


def sum_narrow(value):
    count = lax.axis_size("narrow")
    if count & (count - 1):
        return lax.psum(value, "narrow")
    return butterfly(value, "narrow", [(2 << bit) - 1 for bit in range(count.bit_length() - 1)])


def scatter_wide(parts):
    count = lax.axis_size("wide")
    here = lax.axis_index("wide")
    if count & (count - 1) or count < 2:
        return lax.psum_scatter(parts, "wide", scatter_dimension=0, tiled=False)
    core, chip = lax.rem(here, 2), here // 2
    pairs = parts.reshape(count // 2, 2, *parts.shape[1:])
    mine = lax.dynamic_slice_in_dim(pairs, core, 1, 1)[:, 0]
    other = lax.dynamic_slice_in_dim(pairs, 1 - core, 1, 1)[:, 0]
    summed = mine + exchange(other, "wide", 1)

    def pick(mask):
        return lax.dynamic_slice_in_dim(summed, chip ^ mask, 1, 0)[0]

    got = [exchange(pick(mask), "wide", 2 * mask) for mask in range(1, count // 2)]
    return sum(got, pick(0))


def order_of_groups(local, total):
    used = local.reshape(-1)
    if used.shape[0] == total:
        return used
    ids = jnp.arange(total, dtype=jnp.int32)
    taken = jnp.any(ids[:, None] == used[None, :], axis=1)
    before = (ids[None, :] < ids[:, None]) & ~taken[None, :]
    spot = used.shape[0] + jnp.sum(before.astype(jnp.int32), axis=1)
    slots = jnp.arange(used.shape[0], total, dtype=jnp.int32)
    hit = (spot[None, :] == slots[:, None]) & ~taken[None, :]
    others = jnp.sum(jnp.where(hit, ids[None, :], 0), axis=1).astype(jnp.int32)
    return jnp.concatenate([used, others])


def on_device(
    all_features,
    points,
    scales,
    frequencies,
    phases,
    feature_weights,
    targets,
    noise,
    inverses,
    groups,
):
    wide_count = lax.axis_size("wide")
    narrow_count = lax.axis_size("narrow")
    wide_here = lax.axis_index("wide").astype(jnp.int32)
    narrow_here = lax.axis_index("narrow").astype(jnp.int32)
    shard_groups = points.shape[1] // GROUP
    own = shard_groups // wide_count
    slice_groups = groups.shape[1] // narrow_count
    row_groups = groups.shape[1] // wide_count
    place = jnp.stack(
        [wide_here, narrow_here, jnp.int32(slice_groups), jnp.int32(shard_groups)]
    )
    every = lax.all_gather(points, "narrow", axis=0, tiled=False)
    local = lax.dynamic_slice_in_dim(groups, narrow_here * slice_groups, slice_groups, 1)
    order = order_of_groups(local - narrow_here * shard_groups, shard_groups)
    rows = lax.dynamic_slice_in_dim(groups, wide_here * row_groups, row_groups, 1)
    cuts = [order[:slice_groups], order[slice_groups : 2 * slice_groups], order[2 * slice_groups :]]
    width = slice_groups * GROUP

    prior = functools.partial(
        prior_part,
        place=place,
        own=own,
        factor=math.sqrt(2.0 / all_features),
        freq=frequencies,
        phase=phases[None, :],
        fw=feature_weights,
        points=points,
        targets=targets[None, :],
        noise=noise,
    )
    first = prior(order[:slice_groups], name="prior_first")
    whole = sum_wide(first)
    later = prior(order[slice_groups:], name="prior_later")
    part = inverse_part(whole, inverses, 0, "inverse_0")
    update = sum_narrow(part)
    term = functools.partial(
        kernel_part, place=place, every=every, scales=scales[:, None], own=own
    )
    term_0 = functools.partial(term, rows=rows[0], update=update, block=0, shuffle=False)
    middle = term_0(cuts[1], carry=later[:, :width], start=slice_groups, name="kernel_0_next")
    whole = sum_wide(middle)
    done = [term_0(cuts[0], carry=first, start=0, name="kernel_0_own"), middle]
    if cuts[2].shape[0]:
        done.append(
            term_0(cuts[2], carry=later[:, width:], start=2 * slice_groups, name="kernel_0_rest")
        )
    carry = jnp.concatenate(done, 1)
    part = inverse_part(whole, inverses, 1, "inverse_1")
    update_1 = sum_narrow(part)
    parts = term(
        order,
        rows=rows[1],
        update=update_1,
        carry=carry,
        start=0,
        block=1,
        shuffle=True,
        name="kernel_1",
    )
    return scatter_wide(parts), jnp.stack([update, update_1])


def solution(mesh):
    in_specs = (
        P(None, "narrow"),
        P(),
        P(None, "wide"),
        P("wide"),
        P(None, "wide"),
        P(("narrow", "wide")),
        P(None, ("narrow", "wide")),
        P(None, "wide", "narrow"),
        P(),
    )
    out_specs = (P(None, ("narrow", "wide")), P(None, None, "wide"))

    def run(points, scales, frequencies, *others):
        return jax.shard_map(
            functools.partial(on_device, frequencies.shape[1]),
            mesh=mesh,
            in_specs=in_specs,
            out_specs=out_specs,
            check_vma=False,
        )(points, scales, frequencies, *others)

    return run
```

```python
import functools
import math
from typing import NamedTuple

import jax
import jax.numpy as jnp
from jax import lax
from jax.experimental import pallas as pl
from jax.experimental.pallas import tpu as pltpu
from jax.sharding import PartitionSpec as P

GROUP = 128
BLOCKS = 2
NOISE_VAR = 0.1
LN2 = math.log(2.0)
TO_TURNS = 1.0 / (2.0 * math.pi)
TO_U = math.sqrt(5.0) / LN2
SINE = (-6.283164044164058, 41.33714235333657, -81.34076831835199, 70.99342806157215)
FIRST = 58
F32 = jnp.float32
BF16 = jnp.bfloat16


class Sizes(NamedTuple):
    shard: int
    share: int
    own: int
    rows: int


def thirds(x):
    high = x.astype(BF16).astype(F32)
    rest = x - high
    mid = rest.astype(BF16).astype(F32)
    low = (rest - mid).astype(BF16).astype(F32)
    return high, mid, low


def halves(x):
    high = x.astype(BF16)
    return high, (x - high.astype(F32)).astype(BF16)


def stack_rows(rows):
    width = max(row.shape[1] for row in rows)
    at = lax.broadcasted_iota(jnp.int32, (8, width), 0)
    out = jnp.zeros((8, width), F32)
    for index, row in enumerate(rows):
        out = jnp.where(at == index, row, out)
    return out


def left_terms(parts, extra):
    high, mid, low = parts
    return jnp.concatenate([high, high, mid, mid, high, low, extra, jnp.zeros_like(high)], 0)


def right_terms(parts, extra):
    high, mid, low = parts
    return jnp.concatenate([high, mid, high, mid, low, high, extra, jnp.zeros_like(high)], 0)


def cosine(turns):
    fraction = turns - jnp.round(turns)
    shifted = jnp.abs(fraction) - 0.25
    square = shifted * shifted
    value = SINE[-1]
    for factor in SINE[-2::-1]:
        value = value * square + factor
    return value * shifted


def group_of(ref, index):
    return ref[:, pl.ds(pl.multiple_of(index * GROUP, GROUP), GROUP)]


def dots(terms, high, low, samples):
    both = jnp.dot(terms, high, preferred_element_type=F32)
    return both[:samples] + both[samples:] + jnp.dot(terms[:samples], low, preferred_element_type=F32)


def two_parts(x):
    high, low = halves(x)
    return jnp.concatenate([high, low], 0)


def core_of(side):
    core = lax.rem(lax.axis_index("wide"), 2)
    return core if side else 1 - core


class Block(NamedTuple):
    block: int
    side: int
    begin: int
    count: int

    def at(self, sizes, table, k):
        narrow = lax.axis_index("narrow")
        entry = narrow * sizes.share + core_of(self.side) * (sizes.share // 2) + self.begin + k
        return table[self.block, entry] - narrow * sizes.shard


class Other(NamedTuple):
    begin: int
    count: int

    def at(self, sizes, table, k):
        return table[self.begin + k]


class Natural(NamedTuple):
    side: int
    begin: int
    count: int

    def at(self, sizes, table, k):
        part = self.begin + k // sizes.own
        return (2 * part + core_of(self.side)) * sizes.own + k % sizes.own


def row_group(sizes, table, block, j):
    group = table[block, lax.axis_index("wide") * sizes.rows + j]
    return group // sizes.shard, lax.rem(group, sizes.shard)


def call(body, name, shapes, tables, arrays, flops, after=(), scratch=(), kinds=None, limit=6):
    kinds = kinds or [pltpu.VMEM] * len(arrays)
    spaces = [pltpu.SMEM] * len(tables) + kinds + [pl.ANY] * len(after)

    def run(*refs):
        inputs = len(tables) + len(arrays)
        body(*refs[:inputs], *refs[inputs + len(after) :])

    return pl.pallas_call(
        run,
        out_shape=[jax.ShapeDtypeStruct(*shape) for shape in shapes],
        in_specs=[pl.BlockSpec(memory_space=space) for space in spaces],
        out_specs=[pl.BlockSpec(memory_space=pltpu.VMEM)] * len(shapes),
        scratch_shapes=list(scratch),
        compiler_params=pltpu.CompilerParams(vmem_limit_bytes=limit << 20),
        cost_estimate=pl.CostEstimate(flops=int(flops), bytes_accessed=0, transcendentals=0),
        name=name,
    )(*tables, *arrays, *after)


def prior_tiles(sizes, which, factor, table, left, fw, points, targets, noise, out):
    features, width = left.shape[0], out.shape[1]
    tile, chunk = math.gcd(width, 512), math.gcd(features, 2048)
    per = tile // GROUP
    ones = jnp.ones((1, tile), F32)
    for at in range(width // tile):
        here = slice(at * tile, (at + 1) * tile)
        groups = [which.at(sizes, table, at * per + k) for k in range(per)]
        coords = jnp.concatenate([group_of(points, group) for group in groups], 1)
        right = right_terms(thirds(coords), stack_rows([ones] * 3)).astype(BF16)
        total = jnp.zeros((out.shape[0], tile), F32)
        for begin in range(0, features, chunk):
            cut = slice(begin, begin + chunk)
            turns = jnp.dot(left[cut, :], right, preferred_element_type=F32)
            values = cosine(turns).astype(BF16)
            total += jnp.dot(fw[:, cut], values, preferred_element_type=F32)
        out[:, here] = -factor * total
        for k, group in enumerate(groups):

            @pl.when(group // sizes.own == lax.axis_index("wide"))
            def _():
                inside = lax.rem(group, sizes.own)
                cut = slice(at * tile + k * GROUP, at * tile + (k + 1) * GROUP)
                out[:, cut] += group_of(targets, inside) - group_of(noise, inside)


def first_body(sizes, which, factor, table, *refs):
    sources, (out, left, picked), held, sems = refs[:6], refs[6:9], refs[9:15], refs[15]
    copies = [
        pltpu.make_async_copy(source, target, sems.at[index])
        for index, (source, target) in enumerate(zip(sources, held))
    ]
    for copy in copies:
        copy.start()
    for copy in copies:
        copy.wait()
    freq, phase, fw, points, targets, noise = held
    for block in range(BLOCKS):
        for j in range(sizes.rows):
            owner, inside = row_group(sizes, table, block, j)
            mine = jnp.where(owner == lax.axis_index("narrow"), 1.0, 0.0)
            picked[block, :, j * GROUP : (j + 1) * GROUP] = group_of(points, inside) * mine
    features = freq.shape[1]
    step = math.gcd(features, 512)
    for begin in range(0, features, step):
        cut = slice(begin, begin + step)
        extra = stack_rows(thirds(phase[:, cut] * TO_TURNS))
        terms = left_terms(thirds(freq[:, cut] * TO_TURNS), extra)
        left[cut, :] = terms.T.astype(BF16)
    prior_tiles(sizes, which, factor, table, left, fw, points, targets, noise, out)


def prior_first(sizes, which, factor, table, arrays):
    freq, fw = arrays[0], arrays[2]
    samples, features = fw.shape
    width = which.count * GROUP
    shapes = [
        ((samples, width), F32),
        ((features, 64), BF16),
        ((BLOCKS, freq.shape[0], sizes.rows * GROUP), F32),
    ]
    scratch = [pltpu.VMEM(array.shape, array.dtype) for array in arrays]
    return call(
        functools.partial(first_body, sizes, which, factor),
        "prior_first",
        shapes,
        (table,),
        arrays,
        2300 * features * width,
        scratch=[*scratch, pltpu.SemaphoreType.DMA((len(arrays),))],
        kinds=[pltpu.HBM] * len(arrays),
        limit=FIRST,
    )


def prior_part(sizes, which, factor, table, arrays, name, after=(), cost=800):
    (samples, features), width = arrays[1].shape, which.count * GROUP
    return call(
        functools.partial(prior_tiles, sizes, which, factor),
        name,
        [((samples, width), F32)],
        (table,),
        arrays,
        cost * features * width,
        after,
        limit=14,
    )[0]


def inverse_body(block, side, x, inverses, *refs):
    *before, out = refs
    samples, depth = x.shape
    rows = out.shape[1]
    tile = math.gcd(rows, 512)
    span = pl.ds(pl.multiple_of(core_of(side) * depth, depth), depth)
    high, low = halves(x[...])
    turned = jnp.concatenate([high.astype(F32), low.astype(F32)], 0).T.astype(BF16)
    for row in range(0, rows, tile):
        cut = slice(row, row + tile)
        high, low = halves(inverses[block, cut, span])
        total = jnp.dot(high, turned, preferred_element_type=F32)
        total += jnp.dot(low, turned, preferred_element_type=F32)
        total = total.T
        total = total[:samples] + total[samples:]
        out[:, cut] = total + before[0][:, cut] if before else total


def inverse_part(x, inverses, block, side, before, name):
    rows, depth = inverses.shape[1], x.shape[1]
    return call(
        functools.partial(inverse_body, block, side),
        name,
        [((x.shape[0], rows), F32)],
        (),
        (x, inverses, *before),
        512 * depth * rows,
    )[0]


def add_body(count, *refs):
    terms, outs = refs[: 2 * count], refs[2 * count :]
    rows = [terms[k][...] + terms[count + k][...] for k in range(count)]
    if len(rows) == len(outs):
        for out, row in zip(outs, rows):
            out[...] = row
    elif len(rows) == 1:
        middle = rows[0].shape[0] // 2
        outs[0][...] = rows[0][:middle]
        outs[1][...] = rows[0][middle:]
    else:
        middle = rows[0].shape[0]
        outs[0][:middle] = rows[0]
        outs[0][middle:] = rows[1]


def add(left, right, outs, after, name):
    rows = sum(array.shape[0] for array in left) // outs
    shapes = [((rows, left[0].shape[1]), F32)] * outs
    return call(
        functools.partial(add_body, len(left)), name, shapes, (), (*left, *right), 1e8, after
    )


def kernel_coords(coords, scales):
    centred = (coords - 0.5) * (scales * TO_U)
    return centred, jnp.sum(centred * centred, axis=0, keepdims=True)


def lefts_body(rows, scales, out):
    for block in range(rows.shape[0]):
        for begin in range(0, rows.shape[2], GROUP):
            cut = slice(begin, begin + GROUP)
            centred, norm = kernel_coords(rows[block, :, cut], scales[...])
            ones = jnp.ones((1, GROUP), F32)
            extra = stack_rows([*thirds(norm), ones, ones, ones])
            matrix = left_terms([-2.0 * part for part in thirds(centred)], extra)
            out[block, cut, :] = matrix.T.astype(BF16)


def lefts_part(rows, scales, after):
    shape = (rows.shape[0], rows.shape[2], 64)
    return call(lefts_body, "lefts", [(shape, BF16)], (), (rows, scales), 1e8, after)[0]


def tiles_of(left, right):
    square = jnp.maximum(jnp.dot(left, right, preferred_element_type=F32), 1e-20)
    u = square * lax.rsqrt(square)
    values = (1.0 + u * (LN2 + (LN2 * LN2 / 3.0) * u)) * jnp.exp2(-u)
    return halves(values)


def right_of(sizes, which, table, points, scales, at, per):
    groups = [which.at(sizes, table, at * per + k) for k in range(per)]
    coords = jnp.concatenate([group_of(points, group) for group in groups], 1)
    centred, norm = kernel_coords(coords, scales[...])
    ones = jnp.ones((1, per * GROUP), F32)
    extra = stack_rows([ones, ones, ones, *thirds(norm)])
    return right_terms(thirds(centred), extra).astype(BF16)


def tiles_body(sizes, which, block, table, lefts, points, scales, high_out, low_out):
    depth, width = high_out.shape
    tile, chunk = math.gcd(width, 512), math.gcd(depth, 512)
    for at in range(width // tile):
        right = right_of(sizes, which, table, points, scales, at, tile // GROUP)
        for begin in range(0, depth, chunk):
            cut, here = slice(begin, begin + chunk), slice(at * tile, (at + 1) * tile)
            high, low = tiles_of(lefts[block, cut, :], right)
            high_out[cut, here] = high
            low_out[cut, here] = low


def tiles_part(sizes, which, block, table, lefts, points, scales, name, after=()):
    depth, width = lefts.shape[1], which.count * GROUP
    return call(
        functools.partial(tiles_body, sizes, which, block),
        name,
        [((depth, width), BF16)] * 2,
        (table,),
        (lefts, points, scales),
        1000 * depth * width,
        after,
    )


def product_body(update, high, low, carry, out):
    samples, width = carry.shape
    terms = two_parts(update[...])
    tile = math.gcd(width, 256)
    for begin in range(0, width, tile):
        cut = slice(begin, begin + tile)
        out[:, cut] = carry[:, cut] - dots(terms, high[:, cut], low[:, cut], samples)


def product_part(update, tiles, carry, name):
    flops = 384 * update.shape[1] * carry.shape[1]
    arrays = (update, *tiles, carry)
    return call(product_body, name, [(carry.shape, F32)], (), arrays, flops)[0]


def fused_body(sizes, which, table, lefts, points, scales, update, carry, out):
    samples, width = carry.shape
    depth = lefts.shape[1]
    terms = two_parts(update[...])
    tile, chunk = math.gcd(width, 512), math.gcd(depth, 512)
    for at in range(width // tile):
        here = slice(at * tile, (at + 1) * tile)
        right = right_of(sizes, which, table, points, scales, at, tile // GROUP)
        total = carry[:, here]
        for begin in range(0, depth, chunk):
            cut = slice(begin, begin + chunk)
            total -= dots(terms[:, cut], *tiles_of(lefts[0, cut, :], right), samples)
        out[:, here] = total


def fused_part(sizes, which, table, lefts, points, scales, update, carry, name, after=()):
    return call(
        functools.partial(fused_body, sizes, which),
        name,
        [(carry.shape, F32)],
        (table,),
        (lefts, points, scales, update, carry),
        1600 * lefts.shape[1] * carry.shape[1],
        after,
    )[0]


def group_cut(inside):
    return pl.ds(pl.multiple_of(inside * GROUP, GROUP), GROUP)


def arrange_body(sizes, layout, table, others, update, *refs):
    *pieces, out = refs
    for which, piece in zip(layout, pieces):
        source = others if isinstance(which, Other) else table
        for k in range(which.count):
            group = which.at(sizes, source, k)
            cut = group_cut(lax.rem(group, sizes.own))
            out[group // sizes.own, :, cut] = piece[:, k * GROUP : (k + 1) * GROUP]
    for j in range(sizes.rows):
        owner, inside = row_group(sizes, table, 0, j)

        @pl.when(owner == lax.axis_index("narrow"))
        def _():
            cut = group_cut(lax.rem(inside, sizes.own))
            diagonal = update[:, j * GROUP : (j + 1) * GROUP]
            out[inside // sizes.own, :, cut] -= NOISE_VAR * diagonal


def arrange_part(sizes, layout, table, others, update, pieces, after):
    shape = (sizes.shard // sizes.own, update.shape[0], sizes.own * GROUP)
    return call(
        functools.partial(arrange_body, sizes, layout),
        "arrange",
        [(shape, F32)],
        (table, others),
        (update, *pieces),
        1e8,
        after,
    )[0]


def last_body(sizes, side, table, update, arranged, *refs):
    *tiles, out = refs
    samples = update.shape[0]
    terms = two_parts(update[...])
    core = core_of(side)
    width = sizes.own * GROUP
    tile = math.gcd(width, 256)
    each = out.shape[0] * 2 // len(tiles)
    for part in range(out.shape[0]):
        high, low = tiles[2 * (part // each)], tiles[2 * (part // each) + 1]
        for begin in range(0, width, tile):
            base = (part % each) * width + begin
            cut, here = slice(base, base + tile), slice(begin, begin + tile)
            value = dots(terms, high[:, cut], low[:, cut], samples)
            out[part, :, here] = arranged[2 * part + core, :, here] - value
    for j in range(sizes.rows):
        owner, inside = row_group(sizes, table, 1, j)
        part = inside // sizes.own

        @pl.when((owner == lax.axis_index("narrow")) & (lax.rem(part, 2) == core))
        def _():
            cut = group_cut(lax.rem(inside, sizes.own))
            out[part // 2, :, cut] -= NOISE_VAR * update[:, j * GROUP : (j + 1) * GROUP]


def last_part(sizes, side, table, update, arranged, tiles, name):
    parts, samples, width = arranged.shape
    return call(
        functools.partial(last_body, sizes, side),
        name,
        [((parts // 2, samples, width), F32)],
        (table,),
        (update, arranged, *tiles),
        384 * update.shape[1] * parts * width // 2,
    )[0]


def exchange(value, axis, mask):
    count = lax.axis_size(axis)
    return lax.ppermute(value, axis, [(i, i ^ mask) for i in range(count)])


def butterfly(pair, axis, masks, windows, name):
    steps = list(zip(masks, masks[1:] + masks[:1]))
    for index, (one, two) in enumerate(steps):
        got = exchange(pair[0], axis, one), exchange(pair[1], axis, two)
        beside = windows[index](pair[0]) if index < len(windows) else []
        last = index == len(steps) - 1
        pair = add(pair, got, 1 if last else 2, beside, f"{name}_{index}")
    return pair[0]


def sum_wide(theirs, mine, windows, name):
    count = lax.axis_size("wide")
    pair = add((mine,), (exchange(theirs, "wide", 1),), 2, (), f"{name}_core")
    masks = [1 << bit for bit in range(1, count.bit_length() - 1)]
    return butterfly(pair, "wide", masks, windows, name)


def narrow_masks():
    return [(2 << bit) - 1 for bit in range(lax.axis_size("narrow").bit_length() - 1)]


def sum_narrow(value, windows, name):
    rows = value.shape[0] // 2
    return butterfly((value[:rows], value[rows:]), "narrow", narrow_masks(), windows, name)


def pick_body(mine, got, *outs):
    chip = lax.axis_index("wide") // 2
    for mask, out in enumerate(outs):
        out[...] = mine[chip ^ mask] + got[chip ^ mask]


def scatter_wide(theirs, mine):
    parts, *shape = mine.shape
    got = exchange(theirs, "wide", 1)
    shapes = [(tuple(shape), F32)] * parts
    own, *sent = call(pick_body, "pick", shapes, (), (mine, got), 1e8)
    return sum((exchange(part, "wide", 2 * mask) for mask, part in enumerate(sent, 1)), own)


def other_groups(table, sizes):
    narrow = lax.axis_index("narrow")
    used = lax.dynamic_slice_in_dim(table, narrow * sizes.share, sizes.share, 1).reshape(-1)
    used = used - narrow * sizes.shard
    ids = jnp.arange(sizes.shard, dtype=jnp.int32)
    free = ~jnp.any(ids[:, None] == used[None, :], axis=1)
    before = (ids[None, :] < ids[:, None]) & free[None, :]
    spot = jnp.sum(before.astype(jnp.int32), axis=1)
    slots = jnp.arange(sizes.shard - BLOCKS * sizes.share, dtype=jnp.int32)
    hit = (spot[None, :] == slots[:, None]) & free[None, :]
    return jnp.sum(jnp.where(hit, ids[None, :], 0), axis=1).astype(jnp.int32)


def on_device(
    all_features,
    points,
    scales,
    frequencies,
    phases,
    feature_weights,
    targets,
    noise,
    inverses,
    groups,
):
    wide_count, narrow_count = lax.axis_size("wide"), lax.axis_size("narrow")
    shard_groups = points.shape[1] // GROUP
    sizes = Sizes(
        shard_groups,
        groups.shape[1] // narrow_count,
        shard_groups // wide_count,
        groups.shape[1] // wide_count,
    )
    half = sizes.share // 2
    factor = math.sqrt(2.0 / all_features)
    targets, phases, scales = targets[None, :], phases[None, :], scales[:, None]
    left_over = sizes.shard - BLOCKS * sizes.share
    others = other_groups(groups, sizes) if left_over else groups

    arrays = (frequencies, phases, feature_weights, points, targets, noise)
    halves_0 = [Block(0, side, 0, half) for side in range(2)]
    halves_1 = [Block(1, side, 0, half) for side in range(2)]
    first_theirs, left, picked = prior_first(sizes, halves_0[0], factor, groups, arrays)
    shared = (left, feature_weights, points, targets, noise)
    first_mine = prior_part(
        sizes, halves_0[1], factor, groups, shared, "prior_mine", cost=2300
    )
    flat = picked.reshape(-1, picked.shape[2])

    def row_step(index, after):
        got = exchange(row_sums[-1], "narrow", narrow_masks()[index])
        row_sums.extend(add((row_sums[-1],), (got,), 1, (after,), f"rows_{index}"))

    row_sums = [flat]
    row_step(0, first_mine)

    piece = math.gcd(half, 4)
    pieces = [Block(1, side, begin, piece) for side in range(2) for begin in range(0, half, piece)]
    later = {}

    def prior_beside(chosen, extra, cost):
        def run(after):
            made = []
            for which in chosen:
                name = f"prior_{which.side}_{which.begin}"
                later[which] = prior_part(
                    sizes, which, factor, groups, shared, name, (after,), cost
                )
                made.append(later[which])
            return made + extra(after, made)

        return run

    def weights(mine, block, windows):
        theirs = exchange(mine, "wide", 1)
        part = inverse_part(mine, inverses, block, 1, (), f"inverse_{block}_mine")
        part = inverse_part(theirs, inverses, block, 0, (part,), f"inverse_{block}_theirs")
        return sum_narrow(part, windows, f"narrow_{block}")

    shares = [pieces[k::4] if len(pieces) > 4 else pieces[k : k + 1] for k in range(4)]
    lefts, tiles_0 = [], []

    def rows_beside(after, made):
        for index in range(1, len(narrow_masks())):
            row_step(index, made[-1])
        return row_sums[-1:]

    def lefts_beside(after, made):
        lefts.append(lefts_part(row_sums[-1].reshape(picked.shape), scales, (made[-1],)))
        return lefts

    def tiles_0_beside(side):
        def run(after, made):
            name = f"tiles_0_{side}"
            tiles_0.append(
                tiles_part(
                    sizes, halves_1[side], 0, groups, lefts[0], points, scales, name, (after,)
                )
            )
            return list(tiles_0[-1])

        return run

    extras = [rows_beside, lefts_beside, tiles_0_beside(0), tiles_0_beside(1)]
    costs = [2300, 2300, 800, 800]
    beside = [prior_beside(*terms) for terms in zip(shares, extras, costs)]
    whole = sum_wide(first_theirs, first_mine, beside[:2], "wide_0")
    update = weights(whole, 0, beside[2:])
    carries = [
        jnp.concatenate([later[which] for which in pieces if which.side == side], 1)
        for side in range(2)
    ]
    rest = [Other(begin, piece) for begin in range(0, left_over, piece)]
    rest_prior = [
        prior_part(sizes, which, factor, others, shared, f"prior_rest_{which.begin}")
        for which in rest
    ]
    tiles = functools.partial(tiles_part, sizes, lefts=lefts[0], points=points, scales=scales)
    fused = functools.partial(
        fused_part, sizes, lefts=lefts[0], points=points, scales=scales, update=update
    )
    following = [
        product_part(update, tiles_0[side], carries[side], f"product_0_{side}") for side in range(2)
    ]
    own_pieces = []

    def own_beside(side, carry):
        def run(after):
            name = f"fused_{side}"
            made = fused(halves_0[side], table=groups, carry=carry, name=name, after=(after,))
            own_pieces.append(made)
            return [made]

        return run

    windows = [own_beside(0, first_theirs), own_beside(1, first_mine)]
    whole = sum_wide(*following, windows, "wide_1")
    rest_pieces = [
        fused(which, table=others, carry=carry, name=f"fused_rest_{which.begin}")
        for which, carry in zip(rest, rest_prior)
    ]
    each = max(1, 8 // sizes.own)
    ahead = [[], []]
    arranged = []

    def ahead_beside(side):
        def run(after):
            for begin in range(0, wide_count // 2, each):
                ahead[side] += tiles(
                    Natural(side, begin, each * sizes.own),
                    block=1,
                    table=groups,
                    name=f"tiles_1_{side}_{begin}",
                    after=(after,),
                )
            made = list(ahead[side])
            if side:
                layout = [*halves_0, *halves_1, *rest]
                parts = [*own_pieces, *following, *rest_pieces]
                arranged.append(
                    arrange_part(sizes, layout, groups, others, update, parts, (after,))
                )
                made += arranged
            return made

        return run

    update_1 = weights(whole, 1, [ahead_beside(0), ahead_beside(1)])
    theirs, mine = (
        last_part(sizes, side, groups, update_1, arranged[0], ahead[side], f"last_{side}")
        for side in range(2)
    )
    return scatter_wide(theirs, mine), jnp.stack([update, update_1])


def solution(mesh):
    in_specs = (
        P(None, "narrow"),
        P(),
        P(None, "wide"),
        P("wide"),
        P(None, "wide"),
        P(("narrow", "wide")),
        P(None, ("narrow", "wide")),
        P(None, "wide", "narrow"),
        P(),
    )
    out_specs = (P(None, ("narrow", "wide")), P(None, None, "wide"))

    def run(points, scales, frequencies, *others):
        return jax.shard_map(
            functools.partial(on_device, frequencies.shape[1]),
            mesh=mesh,
            in_specs=in_specs,
            out_specs=out_specs,
            check_vma=False,
        )(points, scales, frequencies, *others)

    return run
```

```python
import functools
import math
from typing import NamedTuple

import jax
import jax.numpy as jnp
from jax import lax
from jax.experimental import pallas as pl
from jax.experimental.pallas import tpu as pltpu
from jax.sharding import PartitionSpec as P

GROUP = 128
BLOCKS = 2
NOISE_VAR = 0.1
LN2 = math.log(2.0)
TO_TURNS = 1.0 / (2.0 * math.pi)
TO_U = math.sqrt(5.0) / LN2
SINE = (-6.283164044164058, 41.33714235333657, -81.34076831835199, 70.99342806157215)
FIRST = 58
F32 = jnp.float32
BF16 = jnp.bfloat16


class Sizes(NamedTuple):
    shard: int
    share: int
    own: int
    rows: int


def thirds(x):
    high = x.astype(BF16).astype(F32)
    rest = x - high
    mid = rest.astype(BF16).astype(F32)
    low = (rest - mid).astype(BF16).astype(F32)
    return high, mid, low


def halves(x):
    high = x.astype(BF16)
    return high, (x - high.astype(F32)).astype(BF16)


def stack_rows(rows):
    width = max(row.shape[1] for row in rows)
    at = lax.broadcasted_iota(jnp.int32, (8, width), 0)
    out = jnp.zeros((8, width), F32)
    for index, row in enumerate(rows):
        out = jnp.where(at == index, row, out)
    return out


def left_terms(parts, extra):
    high, mid, low = parts
    return jnp.concatenate([high, high, mid, mid, high, low, extra, jnp.zeros_like(high)], 0)


def right_terms(parts, extra):
    high, mid, low = parts
    return jnp.concatenate([high, mid, high, mid, low, high, extra, jnp.zeros_like(high)], 0)


def cosine(turns):
    fraction = turns - jnp.round(turns)
    shifted = jnp.abs(fraction) - 0.25
    square = shifted * shifted
    value = SINE[-1]
    for factor in SINE[-2::-1]:
        value = value * square + factor
    return value * shifted


def group_cut(inside):
    return pl.ds(pl.multiple_of(inside * GROUP, GROUP), GROUP)


def group_of(ref, index):
    return ref[:, pl.ds(pl.multiple_of(index * GROUP, GROUP), GROUP)]


def dots(terms, high, low, samples):
    both = jnp.dot(terms, high, preferred_element_type=F32)
    return both[:samples] + both[samples:] + jnp.dot(terms[:samples], low, preferred_element_type=F32)


def two_parts(x):
    high, low = halves(x)
    return jnp.concatenate([high, low], 0)


def core_of(side):
    core = lax.rem(lax.axis_index("wide"), 2)
    return core if side else 1 - core


class Block(NamedTuple):
    block: int
    side: int
    begin: int
    count: int

    def at(self, sizes, table, k):
        narrow = lax.axis_index("narrow")
        entry = narrow * sizes.share + core_of(self.side) * (sizes.share // 2) + self.begin + k
        return table[self.block, entry] - narrow * sizes.shard


class Other(NamedTuple):
    begin: int
    count: int

    def at(self, sizes, table, k):
        return table[self.begin + k]


class Natural(NamedTuple):
    side: int
    begin: int
    count: int

    def at(self, sizes, table, k):
        part = self.begin + k // sizes.own
        return (2 * part + core_of(self.side)) * sizes.own + k % sizes.own


def row_group(sizes, table, block, j):
    group = table[block, lax.axis_index("wide") * sizes.rows + j]
    return group // sizes.shard, lax.rem(group, sizes.shard)


def call(body, name, shapes, tables, arrays, flops, after=(), scratch=(), kinds=None, limit=6):
    kinds = kinds or [pltpu.VMEM] * len(arrays)
    spaces = [pltpu.SMEM] * len(tables) + kinds + [pl.ANY] * len(after)

    def run(*refs):
        inputs = len(tables) + len(arrays)
        body(*refs[:inputs], *refs[inputs + len(after) :])

    return pl.pallas_call(
        run,
        out_shape=[jax.ShapeDtypeStruct(*shape) for shape in shapes],
        in_specs=[pl.BlockSpec(memory_space=space) for space in spaces],
        out_specs=[pl.BlockSpec(memory_space=pltpu.VMEM)] * len(shapes),
        scratch_shapes=list(scratch),
        compiler_params=pltpu.CompilerParams(vmem_limit_bytes=limit << 20),
        cost_estimate=pl.CostEstimate(flops=int(flops), bytes_accessed=0, transcendentals=0),
        name=name,
    )(*tables, *arrays, *after)


def loop(count, body, start=None):
    if count == 1:
        return body(0, start)
    return lax.fori_loop(0, count, body, start)


def prior_tiles(sizes, which, factor, table, left, fw, points, targets, noise, out):
    features, width = left.shape[0], out.shape[1]
    tile, chunk = math.gcd(width, 512), math.gcd(features, 2048)
    per = tile // GROUP
    ones = jnp.ones((1, tile), F32)

    def one_tile(at, _):
        groups = [which.at(sizes, table, at * per + k) for k in range(per)]
        coords = jnp.concatenate([group_of(points, group) for group in groups], 1)
        right = right_terms(thirds(coords), stack_rows([ones] * 3)).astype(BF16)

        def one_chunk(index, total):
            cut = pl.ds(pl.multiple_of(index * chunk, chunk), chunk)
            turns = jnp.dot(left[cut, :], right, preferred_element_type=F32)
            values = cosine(turns).astype(BF16)
            return total + jnp.dot(fw[:, cut], values, preferred_element_type=F32)

        total = loop(features // chunk, one_chunk, jnp.zeros((out.shape[0], tile), F32))
        out[:, pl.ds(pl.multiple_of(at * tile, tile), tile)] = -factor * total
        for k, group in enumerate(groups):

            @pl.when(group // sizes.own == lax.axis_index("wide"))
            def _():
                inside = lax.rem(group, sizes.own)
                out[:, group_cut(at * per + k)] += group_of(targets, inside) - group_of(noise, inside)

        return 0

    loop(width // tile, one_tile, 0)


def first_body(sizes, which, factor, table, *refs):
    sources, (out, left, picked), held, sems = refs[:6], refs[6:9], refs[9:15], refs[15]
    copies = [
        pltpu.make_async_copy(source, target, sems.at[index])
        for index, (source, target) in enumerate(zip(sources, held))
    ]
    for copy in copies:
        copy.start()
    for copy in copies:
        copy.wait()
    freq, phase, fw, points, targets, noise = held
    for block in range(BLOCKS):
        for j in range(sizes.rows):
            owner, inside = row_group(sizes, table, block, j)
            mine = jnp.where(owner == lax.axis_index("narrow"), 1.0, 0.0)
            picked[block, :, j * GROUP : (j + 1) * GROUP] = group_of(points, inside) * mine
    features = freq.shape[1]
    step = math.gcd(features, 512)

    def one_step(index, _):
        cut = pl.ds(pl.multiple_of(index * step, step), step)
        extra = stack_rows(thirds(phase[:, cut] * TO_TURNS))
        terms = left_terms(thirds(freq[:, cut] * TO_TURNS), extra)
        left[cut, :] = terms.T.astype(BF16)
        return 0

    loop(features // step, one_step, 0)
    prior_tiles(sizes, which, factor, table, left, fw, points, targets, noise, out)


def prior_first(sizes, which, factor, table, arrays):
    freq, fw = arrays[0], arrays[2]
    samples, features = fw.shape
    width = which.count * GROUP
    shapes = [
        ((samples, width), F32),
        ((features, 64), BF16),
        ((BLOCKS, freq.shape[0], sizes.rows * GROUP), F32),
    ]
    scratch = [pltpu.VMEM(array.shape, array.dtype) for array in arrays]
    return call(
        functools.partial(first_body, sizes, which, factor),
        "prior_first",
        shapes,
        (table,),
        arrays,
        2300 * features * width,
        scratch=[*scratch, pltpu.SemaphoreType.DMA((len(arrays),))],
        kinds=[pltpu.HBM] * len(arrays),
        limit=FIRST,
    )


def prior_part(sizes, which, factor, table, arrays, name, after=(), cost=800):
    (samples, features), width = arrays[1].shape, which.count * GROUP
    return call(
        functools.partial(prior_tiles, sizes, which, factor),
        name,
        [((samples, width), F32)],
        (table,),
        arrays,
        cost * features * width,
        after,
        limit=14,
    )[0]


def inverse_body(block, side, x, inverses, *refs):
    *before, out = refs
    samples, depth = x.shape
    rows = out.shape[1]
    tile = math.gcd(rows, 512)
    span = pl.ds(pl.multiple_of(core_of(side) * depth, depth), depth)
    high, low = halves(x[...])
    turned = jnp.concatenate([high.astype(F32), low.astype(F32)], 0).T.astype(BF16)
    for row in range(0, rows, tile):
        cut = slice(row, row + tile)
        high, low = halves(inverses[block, cut, span])
        total = jnp.dot(high, turned, preferred_element_type=F32)
        total += jnp.dot(low, turned, preferred_element_type=F32)
        total = total.T
        total = total[:samples] + total[samples:]
        out[:, cut] = total + before[0][:, cut] if before else total


def inverse_part(x, inverses, block, side, before, name):
    rows, depth = inverses.shape[1], x.shape[1]
    return call(
        functools.partial(inverse_body, block, side),
        name,
        [((x.shape[0], rows), F32)],
        (),
        (x, inverses, *before),
        512 * depth * rows,
    )[0]


def add_body(count, *refs):
    terms, outs = refs[: 2 * count], refs[2 * count :]
    rows = [terms[k][...] + terms[count + k][...] for k in range(count)]
    if len(rows) == len(outs):
        for out, row in zip(outs, rows):
            out[...] = row
    elif len(rows) == 1:
        middle = rows[0].shape[0] // 2
        outs[0][...] = rows[0][:middle]
        outs[1][...] = rows[0][middle:]
    else:
        middle = rows[0].shape[0]
        outs[0][:middle] = rows[0]
        outs[0][middle:] = rows[1]


def add(left, right, outs, after, name):
    rows = sum(array.shape[0] for array in left) // outs
    shapes = [((rows, left[0].shape[1]), F32)] * outs
    return call(
        functools.partial(add_body, len(left)), name, shapes, (), (*left, *right), 1e8, after
    )


def kernel_coords(coords, scales):
    centred = (coords - 0.5) * (scales * TO_U)
    return centred, jnp.sum(centred * centred, axis=0, keepdims=True)


def lefts_body(rows, scales, out):
    for block in range(rows.shape[0]):
        for begin in range(0, rows.shape[2], GROUP):
            cut = slice(begin, begin + GROUP)
            centred, norm = kernel_coords(rows[block, :, cut], scales[...])
            ones = jnp.ones((1, GROUP), F32)
            extra = stack_rows([*thirds(norm), ones, ones, ones])
            matrix = left_terms([-2.0 * part for part in thirds(centred)], extra)
            out[block, cut, :] = matrix.T.astype(BF16)


def lefts_part(rows, scales, after):
    shape = (rows.shape[0], rows.shape[2], 64)
    return call(lefts_body, "lefts", [(shape, BF16)], (), (rows, scales), 1e8, after)[0]


def tiles_of(left, right):
    square = jnp.maximum(jnp.dot(left, right, preferred_element_type=F32), 1e-20)
    u = square * lax.rsqrt(square)
    values = (1.0 + u * (LN2 + (LN2 * LN2 / 3.0) * u)) * jnp.exp2(-u)
    return halves(values)


def right_of(sizes, which, table, points, scales, at, per):
    groups = [which.at(sizes, table, at * per + k) for k in range(per)]
    coords = jnp.concatenate([group_of(points, group) for group in groups], 1)
    centred, norm = kernel_coords(coords, scales[...])
    ones = jnp.ones((1, per * GROUP), F32)
    extra = stack_rows([ones, ones, ones, *thirds(norm)])
    return right_terms(thirds(centred), extra).astype(BF16)


def tiles_body(sizes, which, block, table, lefts, points, scales, high_out, low_out):
    depth, width = high_out.shape
    tile = math.gcd(width, 512)

    def one_tile(at, _):
        right = right_of(sizes, which, table, points, scales, at, tile // GROUP)
        here = pl.ds(pl.multiple_of(at * tile, tile), tile)
        high_out[:, here], low_out[:, here] = tiles_of(lefts[block], right)
        return 0

    loop(width // tile, one_tile, 0)


def tiles_part(sizes, which, block, table, lefts, points, scales, name, after=()):
    depth, width = lefts.shape[1], which.count * GROUP
    return call(
        functools.partial(tiles_body, sizes, which, block),
        name,
        [((depth, width), BF16)] * 2,
        (table,),
        (lefts, points, scales),
        300 * depth * width,
        after,
        limit=10,
    )


def product_body(update, high, low, carry, out):
    samples, width = carry.shape
    terms = two_parts(update[...])
    tile = math.gcd(width, 256)
    for begin in range(0, width, tile):
        cut = slice(begin, begin + tile)
        out[:, cut] = carry[:, cut] - dots(terms, high[:, cut], low[:, cut], samples)


def product_part(update, tiles, carry, name):
    flops = 384 * update.shape[1] * carry.shape[1]
    arrays = (update, *tiles, carry)
    return call(product_body, name, [(carry.shape, F32)], (), arrays, flops)[0]


def fused_body(sizes, which, table, lefts, points, scales, update, carry, out):
    samples, width = carry.shape
    terms = two_parts(update[...])
    tile = math.gcd(width, 512)

    def one_tile(at, _):
        right = right_of(sizes, which, table, points, scales, at, tile // GROUP)
        here = pl.ds(pl.multiple_of(at * tile, tile), tile)
        out[:, here] = carry[:, here] - dots(terms, *tiles_of(lefts[0], right), samples)
        return 0

    loop(width // tile, one_tile, 0)


def fused_part(sizes, which, table, lefts, points, scales, update, carry, name, after=()):
    return call(
        functools.partial(fused_body, sizes, which),
        name,
        [(carry.shape, F32)],
        (table,),
        (lefts, points, scales, update, carry),
        1600 * lefts.shape[1] * carry.shape[1],
        after,
        limit=12,
    )[0]


def arrange_body(sizes, layout, table, others, update, *refs):
    *pieces, out = refs
    for which, piece in zip(layout, pieces):
        source = others if isinstance(which, Other) else table
        for k in range(which.count):
            group = which.at(sizes, source, k)
            cut = group_cut(lax.rem(group, sizes.own))
            out[group // sizes.own, :, cut] = piece[:, k * GROUP : (k + 1) * GROUP]
    for j in range(sizes.rows):
        owner, inside = row_group(sizes, table, 0, j)

        @pl.when(owner == lax.axis_index("narrow"))
        def _():
            cut = group_cut(lax.rem(inside, sizes.own))
            diagonal = update[:, j * GROUP : (j + 1) * GROUP]
            out[inside // sizes.own, :, cut] -= NOISE_VAR * diagonal


def arrange_part(sizes, layout, table, others, update, pieces, after):
    shape = (sizes.shard // sizes.own, update.shape[0], sizes.own * GROUP)
    return call(
        functools.partial(arrange_body, sizes, layout),
        "arrange",
        [(shape, F32)],
        (table, others),
        (update, *pieces),
        1e8,
        after,
    )[0]


def last_body(sizes, side, table, update, arranged, *refs):
    *tiles, out = refs
    samples = update.shape[0]
    terms = two_parts(update[...])
    core = core_of(side)
    width = sizes.own * GROUP
    tile = math.gcd(width, 256)
    each = out.shape[0] * 2 // len(tiles)
    for part in range(out.shape[0]):
        high, low = tiles[2 * (part // each)], tiles[2 * (part // each) + 1]
        for begin in range(0, width, tile):
            base = (part % each) * width + begin
            cut, here = slice(base, base + tile), slice(begin, begin + tile)
            value = dots(terms, high[:, cut], low[:, cut], samples)
            out[part, :, here] = arranged[2 * part + core, :, here] - value
    for j in range(sizes.rows):
        owner, inside = row_group(sizes, table, 1, j)
        part = inside // sizes.own

        @pl.when((owner == lax.axis_index("narrow")) & (lax.rem(part, 2) == core))
        def _():
            cut = group_cut(lax.rem(inside, sizes.own))
            out[part // 2, :, cut] -= NOISE_VAR * update[:, j * GROUP : (j + 1) * GROUP]


def last_part(sizes, side, table, update, arranged, tiles, name):
    parts, samples, width = arranged.shape
    return call(
        functools.partial(last_body, sizes, side),
        name,
        [((parts // 2, samples, width), F32)],
        (table,),
        (update, arranged, *tiles),
        384 * update.shape[1] * parts * width // 2,
    )[0]


def exchange(value, axis, mask):
    count = lax.axis_size(axis)
    return lax.ppermute(value, axis, [(i, i ^ mask) for i in range(count)])


def butterfly(pair, axis, masks, windows, name):
    steps = list(zip(masks, masks[1:] + masks[:1]))
    for index, (one, two) in enumerate(steps):
        got = exchange(pair[0], axis, one), exchange(pair[1], axis, two)
        beside = windows[index](pair[0]) if index < len(windows) else []
        last = index == len(steps) - 1
        pair = add(pair, got, 1 if last else 2, beside, f"{name}_{index}")
    return pair[0]


def sum_wide(theirs, mine, windows, name):
    count = lax.axis_size("wide")
    pair = add((mine,), (exchange(theirs, "wide", 1),), 2, (), f"{name}_core")
    masks = [1 << bit for bit in range(1, count.bit_length() - 1)]
    return butterfly(pair, "wide", masks, windows, name)


def narrow_masks():
    return [(2 << bit) - 1 for bit in range(lax.axis_size("narrow").bit_length() - 1)]


def sum_narrow(value, windows, name):
    rows = value.shape[0] // 2
    return butterfly((value[:rows], value[rows:]), "narrow", narrow_masks(), windows, name)


def pick_body(mine, got, *outs):
    chip = lax.axis_index("wide") // 2
    for mask, out in enumerate(outs):
        out[...] = mine[chip ^ mask] + got[chip ^ mask]


def scatter_wide(theirs, mine):
    parts, *shape = mine.shape
    got = exchange(theirs, "wide", 1)
    shapes = [(tuple(shape), F32)] * parts
    own, *sent = call(pick_body, "pick", shapes, (), (mine, got), 1e8)
    return sum((exchange(part, "wide", 2 * mask) for mask, part in enumerate(sent, 1)), own)


def other_groups(table, sizes):
    narrow = lax.axis_index("narrow")
    used = lax.dynamic_slice_in_dim(table, narrow * sizes.share, sizes.share, 1).reshape(-1)
    used = used - narrow * sizes.shard
    ids = jnp.arange(sizes.shard, dtype=jnp.int32)
    free = ~jnp.any(ids[:, None] == used[None, :], axis=1)
    before = (ids[None, :] < ids[:, None]) & free[None, :]
    spot = jnp.sum(before.astype(jnp.int32), axis=1)
    slots = jnp.arange(sizes.shard - BLOCKS * sizes.share, dtype=jnp.int32)
    hit = (spot[None, :] == slots[:, None]) & free[None, :]
    return jnp.sum(jnp.where(hit, ids[None, :], 0), axis=1).astype(jnp.int32)


def on_device(
    all_features,
    points,
    scales,
    frequencies,
    phases,
    feature_weights,
    targets,
    noise,
    inverses,
    groups,
):
    wide_count, narrow_count = lax.axis_size("wide"), lax.axis_size("narrow")
    shard_groups = points.shape[1] // GROUP
    sizes = Sizes(
        shard_groups,
        groups.shape[1] // narrow_count,
        shard_groups // wide_count,
        groups.shape[1] // wide_count,
    )
    half = sizes.share // 2
    factor = math.sqrt(2.0 / all_features)
    targets, phases, scales = targets[None, :], phases[None, :], scales[:, None]
    left_over = sizes.shard - BLOCKS * sizes.share
    others = other_groups(groups, sizes) if left_over else groups

    arrays = (frequencies, phases, feature_weights, points, targets, noise)
    halves_0 = [Block(0, side, 0, half) for side in range(2)]
    halves_1 = [Block(1, side, 0, half) for side in range(2)]
    first_theirs, left, picked = prior_first(sizes, halves_0[0], factor, groups, arrays)
    shared = (left, feature_weights, points, targets, noise)
    first_mine = prior_part(
        sizes, halves_0[1], factor, groups, shared, "prior_mine", cost=2300
    )
    flat = picked.reshape(-1, picked.shape[2])

    def row_step(index, after):
        got = exchange(row_sums[-1], "narrow", narrow_masks()[index])
        row_sums.extend(add((row_sums[-1],), (got,), 1, (after,), f"rows_{index}"))

    row_sums = [flat]
    row_step(0, first_mine)

    piece = math.gcd(half, 4)
    pieces = [Block(1, side, begin, piece) for side in range(2) for begin in range(0, half, piece)]
    later = {}

    def prior_beside(chosen, extra, cost):
        def run(after):
            made = []
            for which in chosen:
                name = f"prior_{which.side}_{which.begin}"
                later[which] = prior_part(
                    sizes, which, factor, groups, shared, name, (after,), cost
                )
                made.append(later[which])
            return made + extra(after, made)

        return run

    def weights(mine, block, windows):
        theirs = exchange(mine, "wide", 1)
        part = inverse_part(mine, inverses, block, 1, (), f"inverse_{block}_mine")
        part = inverse_part(theirs, inverses, block, 0, (part,), f"inverse_{block}_theirs")
        return sum_narrow(part, windows, f"narrow_{block}")

    shares = [pieces[k::4] if len(pieces) > 4 else pieces[k : k + 1] for k in range(4)]
    lefts, tiles_0 = [], []

    def rows_beside(after, made):
        for index in range(1, len(narrow_masks())):
            row_step(index, made[-1])
        return row_sums[-1:]

    def lefts_beside(after, made):
        lefts.append(lefts_part(row_sums[-1].reshape(picked.shape), scales, (made[-1],)))
        return lefts

    def tiles_0_beside(side):
        def run(after, made):
            name = f"tiles_0_{side}"
            tiles_0.append(
                tiles_part(
                    sizes, halves_1[side], 0, groups, lefts[0], points, scales, name, (after,)
                )
            )
            return list(tiles_0[-1])

        return run

    extras = [rows_beside, lefts_beside, tiles_0_beside(0), tiles_0_beside(1)]
    costs = [2300, 2300, 400, 400]
    beside = [prior_beside(*terms) for terms in zip(shares, extras, costs)]
    whole = sum_wide(first_theirs, first_mine, beside[:2], "wide_0")
    update = weights(whole, 0, beside[2:])
    carries = [
        jnp.concatenate([later[which] for which in pieces if which.side == side], 1)
        for side in range(2)
    ]
    rest = [Other(begin, piece) for begin in range(0, left_over, piece)]
    rest_prior = [
        prior_part(sizes, which, factor, others, shared, f"prior_rest_{which.begin}")
        for which in rest
    ]
    tiles = functools.partial(tiles_part, sizes, lefts=lefts[0], points=points, scales=scales)
    fused = functools.partial(
        fused_part, sizes, lefts=lefts[0], points=points, scales=scales, update=update
    )
    following = [
        product_part(update, tiles_0[side], carries[side], f"product_0_{side}") for side in range(2)
    ]
    own_pieces = []

    def own_beside(side, carry):
        def run(after):
            name = f"fused_{side}"
            made = fused(halves_0[side], table=groups, carry=carry, name=name, after=(after,))
            own_pieces.append(made)
            return [made]

        return run

    windows = [own_beside(0, first_theirs), own_beside(1, first_mine)]
    whole = sum_wide(*following, windows, "wide_1")
    rest_pieces = [
        fused(which, table=others, carry=carry, name=f"fused_rest_{which.begin}")
        for which, carry in zip(rest, rest_prior)
    ]
    each = max(1, 8 // sizes.own)
    ahead = [[], []]
    arranged = []

    def ahead_beside(side):
        def run(after):
            for begin in range(0, wide_count // 2, each):
                ahead[side] += tiles(
                    Natural(side, begin, each * sizes.own),
                    block=1,
                    table=groups,
                    name=f"tiles_1_{side}_{begin}",
                    after=(after,),
                )
            made = list(ahead[side])
            if side:
                layout = [*halves_0, *halves_1, *rest]
                parts = [*own_pieces, *following, *rest_pieces]
                arranged.append(
                    arrange_part(sizes, layout, groups, others, update, parts, (after,))
                )
                made += arranged
            return made

        return run

    update_1 = weights(whole, 1, [ahead_beside(0), ahead_beside(1)])
    theirs, mine = (
        last_part(sizes, side, groups, update_1, arranged[0], ahead[side], f"last_{side}")
        for side in range(2)
    )
    return scatter_wide(theirs, mine), jnp.stack([update, update_1])


def solution(mesh):
    in_specs = (
        P(None, "narrow"),
        P(),
        P(None, "wide"),
        P("wide"),
        P(None, "wide"),
        P(("narrow", "wide")),
        P(None, ("narrow", "wide")),
        P(None, "wide", "narrow"),
        P(),
    )
    out_specs = (P(None, ("narrow", "wide")), P(None, None, "wide"))

    def run(points, scales, frequencies, *others):
        return jax.shard_map(
            functools.partial(on_device, frequencies.shape[1]),
            mesh=mesh,
            in_specs=in_specs,
            out_specs=out_specs,
            check_vma=False,
        )(points, scales, frequencies, *others)

    return run
```

```python
import functools
import math
from typing import NamedTuple

import jax
import jax.numpy as jnp
from jax import lax
from jax.experimental import pallas as pl
from jax.experimental.pallas import tpu as pltpu
from jax.sharding import PartitionSpec as P

GROUP = 128
BLOCKS = 2
NOISE_VAR = 0.1
LN2 = math.log(2.0)
TO_TURNS = 1.0 / (2.0 * math.pi)
TO_U = math.sqrt(5.0) / LN2
SINE = (-6.283164044164058, 41.33714235333657, -81.34076831835199, 70.99342806157215)
FIRST = 58
F32 = jnp.float32
BF16 = jnp.bfloat16


class Sizes(NamedTuple):
    shard: int
    share: int
    own: int
    rows: int


def thirds(x):
    high = x.astype(BF16).astype(F32)
    rest = x - high
    mid = rest.astype(BF16).astype(F32)
    low = (rest - mid).astype(BF16).astype(F32)
    return high, mid, low


def halves(x):
    high = x.astype(BF16)
    return high, (x - high.astype(F32)).astype(BF16)


def stack_rows(rows):
    width = max(row.shape[1] for row in rows)
    at = lax.broadcasted_iota(jnp.int32, (8, width), 0)
    out = jnp.zeros((8, width), F32)
    for index, row in enumerate(rows):
        out = jnp.where(at == index, row, out)
    return out


def left_terms(parts, extra):
    high, mid, low = parts
    return jnp.concatenate([high, high, mid, mid, high, low, extra, jnp.zeros_like(high)], 0)


def right_terms(parts, extra):
    high, mid, low = parts
    return jnp.concatenate([high, mid, high, mid, low, high, extra, jnp.zeros_like(high)], 0)


def cosine(turns):
    fraction = turns - jnp.round(turns)
    shifted = jnp.abs(fraction) - 0.25
    square = shifted * shifted
    value = SINE[-1]
    for factor in SINE[-2::-1]:
        value = value * square + factor
    return value * shifted


def group_cut(inside):
    return pl.ds(pl.multiple_of(inside * GROUP, GROUP), GROUP)


def group_of(ref, index):
    return ref[:, pl.ds(pl.multiple_of(index * GROUP, GROUP), GROUP)]


def dots(terms, high, low, samples):
    both = jnp.dot(terms, high, preferred_element_type=F32)
    return both[:samples] + both[samples:] + jnp.dot(terms[:samples], low, preferred_element_type=F32)


def two_parts(x):
    high, low = halves(x)
    return jnp.concatenate([high, low], 0)


def core_of(side):
    core = lax.rem(lax.axis_index("wide"), 2)
    return core if side else 1 - core


class Block(NamedTuple):
    block: int
    side: int
    begin: int
    count: int

    def at(self, sizes, table, k):
        narrow = lax.axis_index("narrow")
        entry = narrow * sizes.share + core_of(self.side) * (sizes.share // 2) + self.begin + k
        return table[self.block, entry] - narrow * sizes.shard


class Other(NamedTuple):
    begin: int
    count: int

    def at(self, sizes, table, k):
        return table[self.begin + k]


class Natural(NamedTuple):
    side: int
    begin: int
    count: int

    def at(self, sizes, table, k):
        part = self.begin + k // sizes.own
        return (2 * part + core_of(self.side)) * sizes.own + k % sizes.own


def row_group(sizes, table, block, j):
    group = table[block, lax.axis_index("wide") * sizes.rows + j]
    return group // sizes.shard, lax.rem(group, sizes.shard)


def call(body, name, shapes, tables, arrays, flops, after=(), scratch=(), kinds=None, limit=6):
    kinds = kinds or [pltpu.VMEM] * len(arrays)
    spaces = [pltpu.SMEM] * len(tables) + kinds + [pl.ANY] * len(after)

    def run(*refs):
        inputs = len(tables) + len(arrays)
        body(*refs[:inputs], *refs[inputs + len(after) :])

    return pl.pallas_call(
        run,
        out_shape=[jax.ShapeDtypeStruct(*shape) for shape in shapes],
        in_specs=[pl.BlockSpec(memory_space=space) for space in spaces],
        out_specs=[pl.BlockSpec(memory_space=pltpu.VMEM)] * len(shapes),
        scratch_shapes=list(scratch),
        compiler_params=pltpu.CompilerParams(vmem_limit_bytes=limit << 20),
        cost_estimate=pl.CostEstimate(flops=int(flops), bytes_accessed=0, transcendentals=0),
        name=name,
    )(*tables, *arrays, *after)


def loop(count, body, start=None):
    if count == 1:
        return body(0, start)
    return lax.fori_loop(0, count, body, start)


def prior_tiles(sizes, which, factor, table, left, fw, points, targets, noise, out):
    features, width = left.shape[0], out.shape[1]
    tile, chunk = math.gcd(width, 512), math.gcd(features, 2048)
    per = tile // GROUP
    ones = jnp.ones((1, tile), F32)

    def one_tile(at, _):
        groups = [which.at(sizes, table, at * per + k) for k in range(per)]
        coords = jnp.concatenate([group_of(points, group) for group in groups], 1)
        right = right_terms(thirds(coords), stack_rows([ones] * 3)).astype(BF16)

        def one_chunk(index, total):
            cut = slice(index * chunk, (index + 1) * chunk)
            turns = jnp.dot(left[cut, :], right, preferred_element_type=F32)
            values = cosine(turns).astype(BF16)
            return total + jnp.dot(fw[:, cut], values, preferred_element_type=F32)

        total = jnp.zeros((out.shape[0], tile), F32)
        for index in range(features // chunk):
            total = one_chunk(index, total)
        out[:, pl.ds(pl.multiple_of(at * tile, tile), tile)] = -factor * total
        for k, group in enumerate(groups):

            @pl.when(group // sizes.own == lax.axis_index("wide"))
            def _():
                inside = lax.rem(group, sizes.own)
                out[:, group_cut(at * per + k)] += group_of(targets, inside) - group_of(noise, inside)

        return 0

    loop(width // tile, one_tile, 0)


def first_body(sizes, which, factor, ratio, table, *refs):
    sources, (out, left, picked), held, sems = refs[:6], refs[6:9], refs[9:15], refs[15]
    copies = [
        pltpu.make_async_copy(source, target, sems.at[index])
        for index, (source, target) in enumerate(zip(sources, held))
    ]
    for copy in copies:
        copy.start()
    freq, phase, points, fw, targets, noise = held
    copies[0].wait()
    copies[1].wait()
    features = freq.shape[1]
    step = math.gcd(features, 512)

    for begin in range(0, features, step):
        cut = slice(begin, begin + step)
        extra = stack_rows(thirds(phase[:, cut] * TO_TURNS))
        terms = left_terms(thirds(freq[:, cut] * TO_TURNS), extra)
        left[cut, :] = terms.T.astype(BF16)
    copies[2].wait()
    narrow, narrow_count = lax.axis_index("narrow"), lax.axis_size("narrow")
    taker = narrow * ratio + lax.axis_index("wide") // narrow_count
    for block in range(BLOCKS):
        for j in range(sizes.rows):
            group = table[block, taker * sizes.rows + j] - narrow * sizes.shard
            picked[block, :, j * GROUP : (j + 1) * GROUP] = group_of(points, group)
    for copy in copies[3:]:
        copy.wait()
    prior_tiles(sizes, which, factor, table, left, fw, points, targets, noise, out)


def prior_first(sizes, which, factor, ratio, table, arrays):
    freq, fw = arrays[0], arrays[3]
    samples, features = fw.shape
    width = which.count * GROUP
    shapes = [
        ((samples, width), F32),
        ((features, 64), BF16),
        ((BLOCKS, freq.shape[0], sizes.rows * GROUP), F32),
    ]
    scratch = [pltpu.VMEM(array.shape, array.dtype) for array in arrays]
    return call(
        functools.partial(first_body, sizes, which, factor, ratio),
        "prior_first",
        shapes,
        (table,),
        arrays,
        2300 * features * width,
        scratch=[*scratch, pltpu.SemaphoreType.DMA((len(arrays),))],
        kinds=[pltpu.HBM] * len(arrays),
        limit=FIRST,
    )


def prior_part(sizes, which, factor, table, arrays, name, after=(), cost=800):
    (samples, features), width = arrays[1].shape, which.count * GROUP
    return call(
        functools.partial(prior_tiles, sizes, which, factor),
        name,
        [((samples, width), F32)],
        (table,),
        arrays,
        cost * features * width,
        after,
        limit=14,
    )[0]


def inverse_body(block, side, x, inverses, *refs):
    *before, out = refs
    samples, depth = x.shape
    rows = out.shape[1]
    tile = math.gcd(rows, 512)
    span = pl.ds(pl.multiple_of(core_of(side) * depth, depth), depth)
    high, low = halves(x[...])
    turned = jnp.concatenate([high.astype(F32), low.astype(F32)], 0).T.astype(BF16)
    for row in range(0, rows, tile):
        cut = slice(row, row + tile)
        high, low = halves(inverses[block, cut, span])
        total = jnp.dot(high, turned, preferred_element_type=F32)
        total += jnp.dot(low, turned, preferred_element_type=F32)
        total = total.T
        total = total[:samples] + total[samples:]
        out[:, cut] = total + before[0][:, cut] if before else total


def inverse_part(x, inverses, block, side, before, name):
    rows, depth = inverses.shape[1], x.shape[1]
    return call(
        functools.partial(inverse_body, block, side),
        name,
        [((x.shape[0], rows), F32)],
        (),
        (x, inverses, *before),
        512 * depth * rows,
    )[0]


def add_body(count, *refs):
    terms, outs = refs[: 2 * count], refs[2 * count :]
    rows = [terms[k][...] + terms[count + k][...] for k in range(count)]
    if len(rows) == len(outs):
        for out, row in zip(outs, rows):
            out[...] = row
    elif len(rows) == 1:
        middle = rows[0].shape[0] // 2
        outs[0][...] = rows[0][:middle]
        outs[1][...] = rows[0][middle:]
    else:
        middle = rows[0].shape[0]
        outs[0][:middle] = rows[0]
        outs[0][middle:] = rows[1]


def add(left, right, outs, after, name):
    rows = sum(array.shape[0] for array in left) // outs
    shapes = [((rows, left[0].shape[1]), F32)] * outs
    return call(
        functools.partial(add_body, len(left)), name, shapes, (), (*left, *right), 1e8, after
    )


def kernel_coords(coords, scales):
    centred = (coords - 0.5) * (scales * TO_U)
    return centred, jnp.sum(centred * centred, axis=0, keepdims=True)


def lefts_body(rows, scales, out):
    for block in range(rows.shape[0]):
        for begin in range(0, rows.shape[2], GROUP):
            cut = slice(begin, begin + GROUP)
            centred, norm = kernel_coords(rows[block, :, cut], scales[...])
            ones = jnp.ones((1, GROUP), F32)
            extra = stack_rows([*thirds(norm), ones, ones, ones])
            matrix = left_terms([-2.0 * part for part in thirds(centred)], extra)
            out[block, cut, :] = matrix.T.astype(BF16)


def lefts_part(rows, scales, after):
    shape = (rows.shape[0], rows.shape[2], 64)
    return call(lefts_body, "lefts", [(shape, BF16)], (), (rows, scales), 1e8, after)[0]


def tiles_of(left, right):
    square = jnp.maximum(jnp.dot(left, right, preferred_element_type=F32), 1e-20)
    u = square * lax.rsqrt(square)
    values = (1.0 + u * (LN2 + (LN2 * LN2 / 3.0) * u)) * jnp.exp2(-u)
    return halves(values)


def right_of(sizes, which, table, points, scales, at, per):
    groups = [which.at(sizes, table, at * per + k) for k in range(per)]
    coords = jnp.concatenate([group_of(points, group) for group in groups], 1)
    centred, norm = kernel_coords(coords, scales[...])
    ones = jnp.ones((1, per * GROUP), F32)
    extra = stack_rows([ones, ones, ones, *thirds(norm)])
    return right_terms(thirds(centred), extra).astype(BF16)


def tiles_body(sizes, which, block, table, lefts, points, scales, high_out, low_out):
    depth, width = high_out.shape
    tile = math.gcd(width, 512)

    def one_tile(at, _):
        right = right_of(sizes, which, table, points, scales, at, tile // GROUP)
        here = pl.ds(pl.multiple_of(at * tile, tile), tile)
        high_out[:, here], low_out[:, here] = tiles_of(lefts[block], right)
        return 0

    loop(width // tile, one_tile, 0)


def tiles_part(sizes, which, block, table, lefts, points, scales, name, after=()):
    depth, width = lefts.shape[1], which.count * GROUP
    return call(
        functools.partial(tiles_body, sizes, which, block),
        name,
        [((depth, width), BF16)] * 2,
        (table,),
        (lefts, points, scales),
        300 * depth * width,
        after,
        limit=10,
    )


def product_body(update, high, low, carry, out):
    samples, width = carry.shape
    terms = two_parts(update[...])
    tile = math.gcd(width, 256)
    for begin in range(0, width, tile):
        cut = slice(begin, begin + tile)
        out[:, cut] = carry[:, cut] - dots(terms, high[:, cut], low[:, cut], samples)


def product_part(update, tiles, carry, name):
    flops = 384 * update.shape[1] * carry.shape[1]
    arrays = (update, *tiles, carry)
    return call(product_body, name, [(carry.shape, F32)], (), arrays, flops)[0]


def fused_body(sizes, which, table, lefts, points, scales, update, carry, out):
    samples, width = carry.shape
    terms = two_parts(update[...])
    tile = math.gcd(width, 512)

    def one_tile(at, _):
        right = right_of(sizes, which, table, points, scales, at, tile // GROUP)
        here = pl.ds(pl.multiple_of(at * tile, tile), tile)
        out[:, here] = carry[:, here] - dots(terms, *tiles_of(lefts[0], right), samples)
        return 0

    loop(width // tile, one_tile, 0)


def fused_part(sizes, which, table, lefts, points, scales, update, carry, name, after=()):
    return call(
        functools.partial(fused_body, sizes, which),
        name,
        [(carry.shape, F32)],
        (table,),
        (lefts, points, scales, update, carry),
        1600 * lefts.shape[1] * carry.shape[1],
        after,
        limit=12,
    )[0]


def arrange_body(sizes, layout, table, others, update, *refs):
    *pieces, out = refs
    for which, piece in zip(layout, pieces):
        source = others if isinstance(which, Other) else table
        for k in range(which.count):
            group = which.at(sizes, source, k)
            cut = group_cut(lax.rem(group, sizes.own))
            out[group // sizes.own, :, cut] = piece[:, k * GROUP : (k + 1) * GROUP]
    for j in range(sizes.rows):
        owner, inside = row_group(sizes, table, 0, j)

        @pl.when(owner == lax.axis_index("narrow"))
        def _():
            cut = group_cut(lax.rem(inside, sizes.own))
            diagonal = update[:, j * GROUP : (j + 1) * GROUP]
            out[inside // sizes.own, :, cut] -= NOISE_VAR * diagonal


def arrange_part(sizes, layout, table, others, update, pieces, after):
    shape = (sizes.shard // sizes.own, update.shape[0], sizes.own * GROUP)
    return call(
        functools.partial(arrange_body, sizes, layout),
        "arrange",
        [(shape, F32)],
        (table, others),
        (update, *pieces),
        1e8,
        after,
    )[0]


def last_body(sizes, side, table, update, arranged, *refs):
    *tiles, out = refs
    samples = update.shape[0]
    terms = two_parts(update[...])
    core = core_of(side)
    width = sizes.own * GROUP
    tile = math.gcd(width, 256)
    each = out.shape[0] * 2 // len(tiles)
    for part in range(out.shape[0]):
        high, low = tiles[2 * (part // each)], tiles[2 * (part // each) + 1]
        for begin in range(0, width, tile):
            base = (part % each) * width + begin
            cut, here = slice(base, base + tile), slice(begin, begin + tile)
            value = dots(terms, high[:, cut], low[:, cut], samples)
            out[part, :, here] = arranged[2 * part + core, :, here] - value
    for j in range(sizes.rows):
        owner, inside = row_group(sizes, table, 1, j)
        part = inside // sizes.own

        @pl.when((owner == lax.axis_index("narrow")) & (lax.rem(part, 2) == core))
        def _():
            cut = group_cut(lax.rem(inside, sizes.own))
            out[part // 2, :, cut] -= NOISE_VAR * update[:, j * GROUP : (j + 1) * GROUP]


def last_part(sizes, side, table, update, arranged, tiles, name):
    parts, samples, width = arranged.shape
    return call(
        functools.partial(last_body, sizes, side),
        name,
        [((parts // 2, samples, width), F32)],
        (table,),
        (update, arranged, *tiles),
        384 * update.shape[1] * parts * width // 2,
    )[0]


def exchange(value, axis, mask):
    count = lax.axis_size(axis)
    return lax.ppermute(value, axis, [(i, i ^ mask) for i in range(count)])


def row_pairs(wide_count, narrow_count):
    ratio = wide_count // narrow_count
    return [
        (((wide % ratio) * narrow_count + narrow) * narrow_count + wide // ratio, wide * narrow_count + narrow)
        for wide in range(wide_count)
        for narrow in range(narrow_count)
    ]


def butterfly(pair, axis, masks, windows, name):
    steps = list(zip(masks, masks[1:] + masks[:1]))
    for index, (one, two) in enumerate(steps):
        got = exchange(pair[0], axis, one), exchange(pair[1], axis, two)
        beside = windows[index](pair[0]) if index < len(windows) else []
        last = index == len(steps) - 1
        pair = add(pair, got, 1 if last else 2, beside, f"{name}_{index}")
    return pair[0]


def sum_wide(theirs, mine, windows, name):
    count = lax.axis_size("wide")
    pair = add((mine,), (exchange(theirs, "wide", 1),), 2, (), f"{name}_core")
    masks = [1 << bit for bit in range(1, count.bit_length() - 1)]
    return butterfly(pair, "wide", masks, windows, name)


def narrow_masks():
    return [(2 << bit) - 1 for bit in range(lax.axis_size("narrow").bit_length() - 1)]


def sum_narrow(value, windows, name):
    rows = value.shape[0] // 2
    return butterfly((value[:rows], value[rows:]), "narrow", narrow_masks(), windows, name)


def pick_body(mine, got, *outs):
    chip = lax.axis_index("wide") // 2
    for mask, out in enumerate(outs):
        out[...] = mine[chip ^ mask] + got[chip ^ mask]


def scatter_wide(theirs, mine):
    parts, *shape = mine.shape
    got = exchange(theirs, "wide", 1)
    shapes = [(tuple(shape), F32)] * parts
    own, *sent = call(pick_body, "pick", shapes, (), (mine, got), 1e8)
    return sum((exchange(part, "wide", 2 * mask) for mask, part in enumerate(sent, 1)), own)


def other_groups(table, sizes):
    narrow = lax.axis_index("narrow")
    used = lax.dynamic_slice_in_dim(table, narrow * sizes.share, sizes.share, 1).reshape(-1)
    used = used - narrow * sizes.shard
    ids = jnp.arange(sizes.shard, dtype=jnp.int32)
    free = ~jnp.any(ids[:, None] == used[None, :], axis=1)
    before = (ids[None, :] < ids[:, None]) & free[None, :]
    spot = jnp.sum(before.astype(jnp.int32), axis=1)
    slots = jnp.arange(sizes.shard - BLOCKS * sizes.share, dtype=jnp.int32)
    hit = (spot[None, :] == slots[:, None]) & free[None, :]
    return jnp.sum(jnp.where(hit, ids[None, :], 0), axis=1).astype(jnp.int32)


def on_device(
    all_features,
    points,
    scales,
    frequencies,
    phases,
    feature_weights,
    targets,
    noise,
    inverses,
    groups,
):
    wide_count, narrow_count = lax.axis_size("wide"), lax.axis_size("narrow")
    shard_groups = points.shape[1] // GROUP
    sizes = Sizes(
        shard_groups,
        groups.shape[1] // narrow_count,
        shard_groups // wide_count,
        groups.shape[1] // wide_count,
    )
    half = sizes.share // 2
    factor = math.sqrt(2.0 / all_features)
    targets, phases, scales = targets[None, :], phases[None, :], scales[:, None]
    left_over = sizes.shard - BLOCKS * sizes.share
    others = other_groups(groups, sizes) if left_over else groups

    arrays = (frequencies, phases, points, feature_weights, targets, noise)
    halves_0 = [Block(0, side, 0, half) for side in range(2)]
    halves_1 = [Block(1, side, 0, half) for side in range(2)]
    ratio = wide_count // narrow_count
    first_theirs, left, picked = prior_first(sizes, halves_0[0], factor, ratio, groups, arrays)
    shared = (left, feature_weights, points, targets, noise)
    first_mine = prior_part(
        sizes, halves_0[1], factor, groups, shared, "prior_mine", cost=2300
    )
    row_points = lax.ppermute(picked, ("wide", "narrow"), row_pairs(wide_count, narrow_count))

    piece = math.gcd(half, 4)
    pieces = [Block(1, side, begin, piece) for side in range(2) for begin in range(0, half, piece)]
    later = {}

    def prior_beside(chosen, extra, cost):
        def run(after):
            made = []
            for which in chosen:
                name = f"prior_{which.side}_{which.begin}"
                later[which] = prior_part(
                    sizes, which, factor, groups, shared, name, (after,), cost
                )
                made.append(later[which])
            return made + extra(after, made)

        return run

    def weights(mine, block, windows):
        theirs = exchange(mine, "wide", 1)
        part = inverse_part(mine, inverses, block, 1, (), f"inverse_{block}_mine")
        part = inverse_part(theirs, inverses, block, 0, (part,), f"inverse_{block}_theirs")
        return sum_narrow(part, windows, f"narrow_{block}")

    shares = [pieces[k::4] if len(pieces) > 4 else pieces[k : k + 1] for k in range(4)]
    lefts, tiles_0 = [], []

    def nothing_beside(after, made):
        return []

    def lefts_beside(after, made):
        lefts.append(lefts_part(row_points, scales, (made[-1],)))
        return lefts

    def tiles_0_beside(side):
        def run(after, made):
            name = f"tiles_0_{side}"
            tiles_0.append(
                tiles_part(
                    sizes, halves_1[side], 0, groups, lefts[0], points, scales, name, (after,)
                )
            )
            return list(tiles_0[-1])

        return run

    extras = [nothing_beside, lefts_beside, tiles_0_beside(0), tiles_0_beside(1)]
    costs = [2300, 2300, 400, 400]
    beside = [prior_beside(*terms) for terms in zip(shares, extras, costs)]
    whole = sum_wide(first_theirs, first_mine, beside[:2], "wide_0")
    update = weights(whole, 0, beside[2:])
    carries = [
        jnp.concatenate([later[which] for which in pieces if which.side == side], 1)
        for side in range(2)
    ]
    rest = [Other(begin, piece) for begin in range(0, left_over, piece)]
    rest_prior = [
        prior_part(sizes, which, factor, others, shared, f"prior_rest_{which.begin}")
        for which in rest
    ]
    tiles = functools.partial(tiles_part, sizes, lefts=lefts[0], points=points, scales=scales)
    fused = functools.partial(
        fused_part, sizes, lefts=lefts[0], points=points, scales=scales, update=update
    )
    following = [
        product_part(update, tiles_0[side], carries[side], f"product_0_{side}") for side in range(2)
    ]
    own_pieces = []

    def own_beside(side, carry):
        def run(after):
            name = f"fused_{side}"
            made = fused(halves_0[side], table=groups, carry=carry, name=name, after=(after,))
            own_pieces.append(made)
            return [made]

        return run

    windows = [own_beside(0, first_theirs), own_beside(1, first_mine)]
    whole = sum_wide(*following, windows, "wide_1")
    rest_pieces = [
        fused(which, table=others, carry=carry, name=f"fused_rest_{which.begin}")
        for which, carry in zip(rest, rest_prior)
    ]
    each = max(1, 8 // sizes.own)
    ahead = [[], []]
    arranged = []

    def ahead_beside(side):
        def run(after):
            for begin in range(0, wide_count // 2, each):
                ahead[side] += tiles(
                    Natural(side, begin, each * sizes.own),
                    block=1,
                    table=groups,
                    name=f"tiles_1_{side}_{begin}",
                    after=(after,),
                )
            made = list(ahead[side])
            if side:
                layout = [*halves_0, *halves_1, *rest]
                parts = [*own_pieces, *following, *rest_pieces]
                arranged.append(
                    arrange_part(sizes, layout, groups, others, update, parts, (after,))
                )
                made += arranged
            return made

        return run

    update_1 = weights(whole, 1, [ahead_beside(0), ahead_beside(1)])
    theirs, mine = (
        last_part(sizes, side, groups, update_1, arranged[0], ahead[side], f"last_{side}")
        for side in range(2)
    )
    return scatter_wide(theirs, mine), jnp.stack([update, update_1])


def solution(mesh):
    in_specs = (
        P(None, "narrow"),
        P(),
        P(None, "wide"),
        P("wide"),
        P(None, "wide"),
        P(("narrow", "wide")),
        P(None, ("narrow", "wide")),
        P(None, "wide", "narrow"),
        P(),
    )
    out_specs = (P(None, ("narrow", "wide")), P(None, None, "wide"))

    def run(points, scales, frequencies, *others):
        return jax.shard_map(
            functools.partial(on_device, frequencies.shape[1]),
            mesh=mesh,
            in_specs=in_specs,
            out_specs=out_specs,
            check_vma=False,
        )(points, scales, frequencies, *others)

    return run
```

```python
import functools
import math
from typing import NamedTuple

import jax
import jax.numpy as jnp
from jax import lax
from jax.experimental import pallas as pl
from jax.experimental.pallas import tpu as pltpu
from jax.sharding import PartitionSpec as P

GROUP = 128
BLOCKS = 2
NOISE_VAR = 0.1
LN2 = math.log(2.0)
TO_TURNS = 1.0 / (2.0 * math.pi)
TO_U = math.sqrt(5.0) / LN2
SINE = (-6.283164044164058, 41.33714235333657, -81.34076831835199, 70.99342806157215)
FIRST = 58
F32 = jnp.float32
BF16 = jnp.bfloat16


class Sizes(NamedTuple):
    shard: int
    share: int
    own: int
    rows: int


def thirds(x):
    high = x.astype(BF16).astype(F32)
    rest = x - high
    mid = rest.astype(BF16).astype(F32)
    low = (rest - mid).astype(BF16).astype(F32)
    return high, mid, low


def halves(x):
    high = x.astype(BF16)
    return high, (x - high.astype(F32)).astype(BF16)


def stack_rows(rows):
    width = max(row.shape[1] for row in rows)
    at = lax.broadcasted_iota(jnp.int32, (8, width), 0)
    out = jnp.zeros((8, width), F32)
    for index, row in enumerate(rows):
        out = jnp.where(at == index, row, out)
    return out


def left_terms(parts, extra):
    high, mid, low = parts
    return jnp.concatenate([high, high, mid, mid, high, low, extra, jnp.zeros_like(high)], 0)


def right_terms(parts, extra):
    high, mid, low = parts
    return jnp.concatenate([high, mid, high, mid, low, high, extra, jnp.zeros_like(high)], 0)


def cosine(turns):
    fraction = turns - jnp.round(turns)
    shifted = jnp.abs(fraction) - 0.25
    square = shifted * shifted
    value = SINE[-1]
    for factor in SINE[-2::-1]:
        value = value * square + factor
    return value * shifted


def group_cut(inside):
    return pl.ds(pl.multiple_of(inside * GROUP, GROUP), GROUP)


def group_of(ref, index):
    return ref[:, pl.ds(pl.multiple_of(index * GROUP, GROUP), GROUP)]


def dots(terms, high, low, samples):
    both = jnp.dot(terms, high, preferred_element_type=F32)
    return both[:samples] + both[samples:] + jnp.dot(terms[:samples], low, preferred_element_type=F32)


def two_parts(x):
    high, low = halves(x)
    return jnp.concatenate([high, low], 0)


def core_of(side):
    core = lax.rem(lax.axis_index("wide"), 2)
    return core if side else 1 - core


class Block(NamedTuple):
    block: int
    side: int
    begin: int
    count: int

    def at(self, sizes, table, k):
        narrow = lax.axis_index("narrow")
        entry = narrow * sizes.share + core_of(self.side) * (sizes.share // 2) + self.begin + k
        return table[self.block, entry] - narrow * sizes.shard


class Other(NamedTuple):
    begin: int
    count: int

    def at(self, sizes, table, k):
        return table[self.begin + k]


class Natural(NamedTuple):
    side: int
    begin: int
    count: int

    def at(self, sizes, table, k):
        part = self.begin + k // sizes.own
        return (2 * part + core_of(self.side)) * sizes.own + k % sizes.own


def row_group(sizes, table, block, j):
    group = table[block, lax.axis_index("wide") * sizes.rows + j]
    return group // sizes.shard, lax.rem(group, sizes.shard)


def call(body, name, shapes, tables, arrays, flops, after=(), scratch=(), kinds=None, limit=6):
    kinds = kinds or [pltpu.VMEM] * len(arrays)
    spaces = [pltpu.SMEM] * len(tables) + kinds + [pl.ANY] * len(after)

    def run(*refs):
        inputs = len(tables) + len(arrays)
        body(*refs[:inputs], *refs[inputs + len(after) :])

    return pl.pallas_call(
        run,
        out_shape=[jax.ShapeDtypeStruct(*shape) for shape in shapes],
        in_specs=[pl.BlockSpec(memory_space=space) for space in spaces],
        out_specs=[pl.BlockSpec(memory_space=pltpu.VMEM)] * len(shapes),
        scratch_shapes=list(scratch),
        compiler_params=pltpu.CompilerParams(vmem_limit_bytes=limit << 20),
        cost_estimate=pl.CostEstimate(flops=int(flops), bytes_accessed=0, transcendentals=0),
        name=name,
    )(*tables, *arrays, *after)


def loop(count, body, start=None):
    if count == 1:
        return body(0, start)
    return lax.fori_loop(0, count, body, start)


def prior_tiles(sizes, which, factor, table, left, fw, points, targets, noise, out):
    features, width = left.shape[0], out.shape[1]
    tile, chunk = math.gcd(width, 512), math.gcd(features, 2048)
    per = tile // GROUP
    ones = jnp.ones((1, tile), F32)

    def one_tile(at, _):
        groups = [which.at(sizes, table, at * per + k) for k in range(per)]
        coords = jnp.concatenate([group_of(points, group) for group in groups], 1)
        right = right_terms(thirds(coords), stack_rows([ones] * 3)).astype(BF16)

        def one_chunk(index, total):
            cut = pl.ds(pl.multiple_of(index * chunk, chunk), chunk)
            turns = jnp.dot(left[cut, :], right, preferred_element_type=F32)
            values = cosine(turns).astype(BF16)
            return total + jnp.dot(fw[:, cut], values, preferred_element_type=F32)

        total = jnp.zeros((out.shape[0], tile), F32)
        if width > tile:
            for index in range(features // chunk):
                total = one_chunk(index, total)
        else:
            total = loop(features // chunk, one_chunk, total)
        out[:, pl.ds(pl.multiple_of(at * tile, tile), tile)] = -factor * total
        for k, group in enumerate(groups):

            @pl.when(group // sizes.own == lax.axis_index("wide"))
            def _():
                inside = lax.rem(group, sizes.own)
                out[:, group_cut(at * per + k)] += group_of(targets, inside) - group_of(noise, inside)

        return 0

    loop(width // tile, one_tile, 0)


def first_body(sizes, which, factor, table, *refs):
    sources, (out, left, picked), held, sems = refs[:6], refs[6:9], refs[9:15], refs[15]
    copies = [
        pltpu.make_async_copy(source, target, sems.at[index])
        for index, (source, target) in enumerate(zip(sources, held))
    ]
    for copy in copies:
        copy.start()
    freq, phase, points, fw, targets, noise = held
    copies[0].wait()
    copies[1].wait()
    features = freq.shape[1]
    step = math.gcd(features, 1024)

    def one_step(index, _):
        cut = pl.ds(pl.multiple_of(index * step, step), step)
        extra = stack_rows(thirds(phase[:, cut] * TO_TURNS))
        terms = left_terms(thirds(freq[:, cut] * TO_TURNS), extra)
        left[cut, :] = terms.T.astype(BF16)
        return 0

    loop(features // step, one_step, 0)
    copies[2].wait()
    for block in range(BLOCKS):
        for j in range(sizes.rows):
            owner, inside = row_group(sizes, table, block, j)
            mine = jnp.where(owner == lax.axis_index("narrow"), 1.0, 0.0)
            picked[block, :, j * GROUP : (j + 1) * GROUP] = group_of(points, inside) * mine
    for copy in copies[3:]:
        copy.wait()
    prior_tiles(sizes, which, factor, table, left, fw, points, targets, noise, out)


def prior_first(sizes, which, factor, table, arrays):
    freq, fw = arrays[0], arrays[3]
    samples, features = fw.shape
    width = which.count * GROUP
    shapes = [
        ((samples, width), F32),
        ((features, 64), BF16),
        ((BLOCKS, freq.shape[0], sizes.rows * GROUP), F32),
    ]
    scratch = [pltpu.VMEM(array.shape, array.dtype) for array in arrays]
    return call(
        functools.partial(first_body, sizes, which, factor),
        "prior_first",
        shapes,
        (table,),
        arrays,
        2300 * features * width,
        scratch=[*scratch, pltpu.SemaphoreType.DMA((len(arrays),))],
        kinds=[pltpu.HBM] * len(arrays),
        limit=FIRST,
    )


def prior_part(sizes, which, factor, table, arrays, name, after=(), cost=800):
    (samples, features), width = arrays[1].shape, which.count * GROUP
    return call(
        functools.partial(prior_tiles, sizes, which, factor),
        name,
        [((samples, width), F32)],
        (table,),
        arrays,
        cost * features * width,
        after,
        limit=14,
    )[0]


def inverse_body(block, side, x, inverses, *refs):
    *before, out = refs
    samples, depth = x.shape
    rows = out.shape[1]
    tile = math.gcd(rows, 512)
    span = pl.ds(pl.multiple_of(core_of(side) * depth, depth), depth)
    high, low = halves(x[...])
    turned = jnp.concatenate([high.astype(F32), low.astype(F32)], 0).T.astype(BF16)
    for row in range(0, rows, tile):
        cut = slice(row, row + tile)
        high, low = halves(inverses[block, cut, span])
        total = jnp.dot(high, turned, preferred_element_type=F32)
        total += jnp.dot(low, turned, preferred_element_type=F32)
        total = total.T
        total = total[:samples] + total[samples:]
        out[:, cut] = total + before[0][:, cut] if before else total


def inverse_part(x, inverses, block, side, before, name):
    rows, depth = inverses.shape[1], x.shape[1]
    return call(
        functools.partial(inverse_body, block, side),
        name,
        [((x.shape[0], rows), F32)],
        (),
        (x, inverses, *before),
        512 * depth * rows,
    )[0]


def add_body(count, *refs):
    terms, outs = refs[: 2 * count], refs[2 * count :]
    rows = [terms[k][...] + terms[count + k][...] for k in range(count)]
    if len(rows) == len(outs):
        for out, row in zip(outs, rows):
            out[...] = row
    elif len(rows) == 1:
        middle = rows[0].shape[0] // 2
        outs[0][...] = rows[0][:middle]
        outs[1][...] = rows[0][middle:]
    else:
        middle = rows[0].shape[0]
        outs[0][:middle] = rows[0]
        outs[0][middle:] = rows[1]


def add(left, right, outs, after, name):
    rows = sum(array.shape[0] for array in left) // outs
    shapes = [((rows, left[0].shape[1]), F32)] * outs
    return call(
        functools.partial(add_body, len(left)), name, shapes, (), (*left, *right), 1e8, after
    )


def kernel_coords(coords, scales):
    centred = (coords - 0.5) * (scales * TO_U)
    return centred, jnp.sum(centred * centred, axis=0, keepdims=True)


def lefts_body(rows, scales, out):
    for block in range(rows.shape[0]):
        for begin in range(0, rows.shape[2], GROUP):
            cut = slice(begin, begin + GROUP)
            centred, norm = kernel_coords(rows[block, :, cut], scales[...])
            ones = jnp.ones((1, GROUP), F32)
            extra = stack_rows([*thirds(norm), ones, ones, ones])
            matrix = left_terms([-2.0 * part for part in thirds(centred)], extra)
            out[block, cut, :] = matrix.T.astype(BF16)


def lefts_part(rows, scales, after):
    shape = (rows.shape[0], rows.shape[2], 64)
    return call(lefts_body, "lefts", [(shape, BF16)], (), (rows, scales), 1e8, after)[0]


def tiles_of(left, right):
    square = jnp.maximum(jnp.dot(left, right, preferred_element_type=F32), 1e-20)
    u = square * lax.rsqrt(square)
    values = (1.0 + u * (LN2 + (LN2 * LN2 / 3.0) * u)) * jnp.exp2(-u)
    return halves(values)


def right_of(sizes, which, table, points, scales, at, per):
    groups = [which.at(sizes, table, at * per + k) for k in range(per)]
    coords = jnp.concatenate([group_of(points, group) for group in groups], 1)
    centred, norm = kernel_coords(coords, scales[...])
    ones = jnp.ones((1, per * GROUP), F32)
    extra = stack_rows([ones, ones, ones, *thirds(norm)])
    return right_terms(thirds(centred), extra).astype(BF16)


def tiles_body(sizes, which, block, table, lefts, points, scales, high_out, low_out):
    depth, width = high_out.shape
    tile = math.gcd(width, 512)

    def one_tile(at, _):
        right = right_of(sizes, which, table, points, scales, at, tile // GROUP)
        here = pl.ds(pl.multiple_of(at * tile, tile), tile)
        high_out[:, here], low_out[:, here] = tiles_of(lefts[block], right)
        return 0

    loop(width // tile, one_tile, 0)


def tiles_part(sizes, which, block, table, lefts, points, scales, name, after=()):
    depth, width = lefts.shape[1], which.count * GROUP
    return call(
        functools.partial(tiles_body, sizes, which, block),
        name,
        [((depth, width), BF16)] * 2,
        (table,),
        (lefts, points, scales),
        300 * depth * width,
        after,
        limit=10,
    )


def product_body(update, high, low, carry, out):
    samples, width = carry.shape
    terms = two_parts(update[...])
    tile = math.gcd(width, 256)
    for begin in range(0, width, tile):
        cut = slice(begin, begin + tile)
        out[:, cut] = carry[:, cut] - dots(terms, high[:, cut], low[:, cut], samples)


def product_part(update, tiles, carry, name):
    flops = 384 * update.shape[1] * carry.shape[1]
    arrays = (update, *tiles, carry)
    return call(product_body, name, [(carry.shape, F32)], (), arrays, flops)[0]


def fused_body(sizes, which, table, lefts, points, scales, update, carry, out):
    samples, width = carry.shape
    terms = two_parts(update[...])
    tile = math.gcd(width, 512)

    def one_tile(at, _):
        right = right_of(sizes, which, table, points, scales, at, tile // GROUP)
        here = pl.ds(pl.multiple_of(at * tile, tile), tile)
        out[:, here] = carry[:, here] - dots(terms, *tiles_of(lefts[0], right), samples)
        return 0

    loop(width // tile, one_tile, 0)


def fused_part(sizes, which, table, lefts, points, scales, update, carry, name, after=()):
    return call(
        functools.partial(fused_body, sizes, which),
        name,
        [(carry.shape, F32)],
        (table,),
        (lefts, points, scales, update, carry),
        1600 * lefts.shape[1] * carry.shape[1],
        after,
        limit=12,
    )[0]


def arrange_body(sizes, layout, table, others, update, *refs):
    *pieces, out = refs
    for which, piece in zip(layout, pieces):
        source = others if isinstance(which, Other) else table
        for k in range(which.count):
            group = which.at(sizes, source, k)
            cut = group_cut(lax.rem(group, sizes.own))
            out[group // sizes.own, :, cut] = piece[:, k * GROUP : (k + 1) * GROUP]
    for j in range(sizes.rows):
        owner, inside = row_group(sizes, table, 0, j)

        @pl.when(owner == lax.axis_index("narrow"))
        def _():
            cut = group_cut(lax.rem(inside, sizes.own))
            diagonal = update[:, j * GROUP : (j + 1) * GROUP]
            out[inside // sizes.own, :, cut] -= NOISE_VAR * diagonal


def arrange_part(sizes, layout, table, others, update, pieces, after):
    shape = (sizes.shard // sizes.own, update.shape[0], sizes.own * GROUP)
    return call(
        functools.partial(arrange_body, sizes, layout),
        "arrange",
        [(shape, F32)],
        (table, others),
        (update, *pieces),
        1e8,
        after,
    )[0]


def last_body(sizes, side, table, update, arranged, *refs):
    *tiles, out = refs
    samples = update.shape[0]
    terms = two_parts(update[...])
    core = core_of(side)
    width = sizes.own * GROUP
    tile = math.gcd(width, 256)
    each = out.shape[0] * 2 // len(tiles)
    for part in range(out.shape[0]):
        high, low = tiles[2 * (part // each)], tiles[2 * (part // each) + 1]
        for begin in range(0, width, tile):
            base = (part % each) * width + begin
            cut, here = slice(base, base + tile), slice(begin, begin + tile)
            value = dots(terms, high[:, cut], low[:, cut], samples)
            out[part, :, here] = arranged[2 * part + core, :, here] - value
    for j in range(sizes.rows):
        owner, inside = row_group(sizes, table, 1, j)
        part = inside // sizes.own

        @pl.when((owner == lax.axis_index("narrow")) & (lax.rem(part, 2) == core))
        def _():
            cut = group_cut(lax.rem(inside, sizes.own))
            out[part // 2, :, cut] -= NOISE_VAR * update[:, j * GROUP : (j + 1) * GROUP]


def last_part(sizes, side, table, update, arranged, tiles, name):
    parts, samples, width = arranged.shape
    return call(
        functools.partial(last_body, sizes, side),
        name,
        [((parts // 2, samples, width), F32)],
        (table,),
        (update, arranged, *tiles),
        384 * update.shape[1] * parts * width // 2,
    )[0]


def exchange(value, axis, mask):
    count = lax.axis_size(axis)
    return lax.ppermute(value, axis, [(i, i ^ mask) for i in range(count)])


def butterfly(pair, axis, masks, windows, name):
    steps = list(zip(masks, masks[1:] + masks[:1]))
    for index, (one, two) in enumerate(steps):
        got = exchange(pair[0], axis, one), exchange(pair[1], axis, two)
        beside = windows[index](pair[0]) if index < len(windows) else []
        last = index == len(steps) - 1
        pair = add(pair, got, 1 if last else 2, beside, f"{name}_{index}")
    return pair[0]


def sum_wide(theirs, mine, windows, name):
    count = lax.axis_size("wide")
    pair = add((mine,), (exchange(theirs, "wide", 1),), 2, (), f"{name}_core")
    masks = [1 << bit for bit in range(1, count.bit_length() - 1)]
    return butterfly(pair, "wide", masks, windows, name)


def narrow_masks():
    return [(2 << bit) - 1 for bit in range(lax.axis_size("narrow").bit_length() - 1)]


def sum_narrow(value, windows, name):
    rows = value.shape[0] // 2
    return butterfly((value[:rows], value[rows:]), "narrow", narrow_masks(), windows, name)


def pick_body(mine, got, *outs):
    chip = lax.axis_index("wide") // 2
    for mask, out in enumerate(outs):
        out[...] = mine[chip ^ mask] + got[chip ^ mask]


def scatter_wide(theirs, mine):
    parts, *shape = mine.shape
    got = exchange(theirs, "wide", 1)
    shapes = [(tuple(shape), F32)] * parts
    own, *sent = call(pick_body, "pick", shapes, (), (mine, got), 1e8)
    return sum((exchange(part, "wide", 2 * mask) for mask, part in enumerate(sent, 1)), own)


def other_groups(table, sizes):
    narrow = lax.axis_index("narrow")
    used = lax.dynamic_slice_in_dim(table, narrow * sizes.share, sizes.share, 1).reshape(-1)
    used = used - narrow * sizes.shard
    ids = jnp.arange(sizes.shard, dtype=jnp.int32)
    free = ~jnp.any(ids[:, None] == used[None, :], axis=1)
    before = (ids[None, :] < ids[:, None]) & free[None, :]
    spot = jnp.sum(before.astype(jnp.int32), axis=1)
    slots = jnp.arange(sizes.shard - BLOCKS * sizes.share, dtype=jnp.int32)
    hit = (spot[None, :] == slots[:, None]) & free[None, :]
    return jnp.sum(jnp.where(hit, ids[None, :], 0), axis=1).astype(jnp.int32)


def on_device(
    all_features,
    points,
    scales,
    frequencies,
    phases,
    feature_weights,
    targets,
    noise,
    inverses,
    groups,
):
    wide_count, narrow_count = lax.axis_size("wide"), lax.axis_size("narrow")
    shard_groups = points.shape[1] // GROUP
    sizes = Sizes(
        shard_groups,
        groups.shape[1] // narrow_count,
        shard_groups // wide_count,
        groups.shape[1] // wide_count,
    )
    half = sizes.share // 2
    factor = math.sqrt(2.0 / all_features)
    targets, phases, scales = targets[None, :], phases[None, :], scales[:, None]
    left_over = sizes.shard - BLOCKS * sizes.share
    others = other_groups(groups, sizes) if left_over else groups

    arrays = (frequencies, phases, points, feature_weights, targets, noise)
    halves_0 = [Block(0, side, 0, half) for side in range(2)]
    halves_1 = [Block(1, side, 0, half) for side in range(2)]
    first_theirs, left, picked = prior_first(sizes, halves_0[0], factor, groups, arrays)
    shared = (left, feature_weights, points, targets, noise)
    first_mine = prior_part(
        sizes, halves_0[1], factor, groups, shared, "prior_mine", cost=2300
    )
    flat = picked.reshape(-1, picked.shape[2])

    def row_step(index, after):
        got = exchange(row_sums[-1], "narrow", narrow_masks()[index])
        row_sums.extend(add((row_sums[-1],), (got,), 1, (after,), f"rows_{index}"))

    row_sums = [flat]
    row_step(0, first_mine)

    piece = math.gcd(half, 4)
    pieces = [Block(1, side, begin, piece) for side in range(2) for begin in range(0, half, piece)]
    later = {}

    def prior_beside(chosen, extra, cost):
        def run(after):
            made = []
            for which in chosen:
                name = f"prior_{which.side}_{which.begin}"
                later[which] = prior_part(
                    sizes, which, factor, groups, shared, name, (after,), cost
                )
                made.append(later[which])
            return made + extra(after, made)

        return run

    def weights(mine, block, windows):
        theirs = exchange(mine, "wide", 1)
        part = inverse_part(mine, inverses, block, 1, (), f"inverse_{block}_mine")
        part = inverse_part(theirs, inverses, block, 0, (part,), f"inverse_{block}_theirs")
        return sum_narrow(part, windows, f"narrow_{block}")

    shares = [pieces[k::4] if len(pieces) > 4 else pieces[k : k + 1] for k in range(4)]
    lefts, tiles_0 = [], []

    def rows_beside(after, made):
        for index in range(1, len(narrow_masks())):
            row_step(index, made[-1])
        return row_sums[-1:]

    def lefts_beside(after, made):
        lefts.append(lefts_part(row_sums[-1].reshape(picked.shape), scales, (made[-1],)))
        return lefts

    def tiles_0_beside(side):
        def run(after, made):
            name = f"tiles_0_{side}"
            tiles_0.append(
                tiles_part(
                    sizes, halves_1[side], 0, groups, lefts[0], points, scales, name, (after,)
                )
            )
            return list(tiles_0[-1])

        return run

    extras = [rows_beside, lefts_beside, tiles_0_beside(0), tiles_0_beside(1)]
    costs = [2300, 2300, 400, 400]
    beside = [prior_beside(*terms) for terms in zip(shares, extras, costs)]
    whole = sum_wide(first_theirs, first_mine, beside[:2], "wide_0")
    update = weights(whole, 0, beside[2:])
    carries = [
        jnp.concatenate([later[which] for which in pieces if which.side == side], 1)
        for side in range(2)
    ]
    rest = [Other(begin, piece) for begin in range(0, left_over, piece)]
    rest_prior = [
        prior_part(sizes, which, factor, others, shared, f"prior_rest_{which.begin}")
        for which in rest
    ]
    tiles = functools.partial(tiles_part, sizes, lefts=lefts[0], points=points, scales=scales)
    fused = functools.partial(
        fused_part, sizes, lefts=lefts[0], points=points, scales=scales, update=update
    )
    following = [
        product_part(update, tiles_0[side], carries[side], f"product_0_{side}") for side in range(2)
    ]
    own_pieces = []

    def own_beside(side, carry):
        def run(after):
            name = f"fused_{side}"
            made = fused(halves_0[side], table=groups, carry=carry, name=name, after=(after,))
            own_pieces.append(made)
            return [made]

        return run

    windows = [own_beside(0, first_theirs), own_beside(1, first_mine)]
    whole = sum_wide(*following, windows, "wide_1")
    rest_pieces = [
        fused(which, table=others, carry=carry, name=f"fused_rest_{which.begin}")
        for which, carry in zip(rest, rest_prior)
    ]
    each = max(1, 8 // sizes.own)
    ahead = [[], []]
    arranged = []

    def ahead_beside(side):
        def run(after):
            for begin in range(0, wide_count // 2, each):
                ahead[side] += tiles(
                    Natural(side, begin, each * sizes.own),
                    block=1,
                    table=groups,
                    name=f"tiles_1_{side}_{begin}",
                    after=(after,),
                )
            made = list(ahead[side])
            if side:
                layout = [*halves_0, *halves_1, *rest]
                parts = [*own_pieces, *following, *rest_pieces]
                arranged.append(
                    arrange_part(sizes, layout, groups, others, update, parts, (after,))
                )
                made += arranged
            return made

        return run

    update_1 = weights(whole, 1, [ahead_beside(0), ahead_beside(1)])
    theirs, mine = (
        last_part(sizes, side, groups, update_1, arranged[0], ahead[side], f"last_{side}")
        for side in range(2)
    )
    return scatter_wide(theirs, mine), jnp.stack([update, update_1])


def solution(mesh):
    in_specs = (
        P(None, "narrow"),
        P(),
        P(None, "wide"),
        P("wide"),
        P(None, "wide"),
        P(("narrow", "wide")),
        P(None, ("narrow", "wide")),
        P(None, "wide", "narrow"),
        P(),
    )
    out_specs = (P(None, ("narrow", "wide")), P(None, None, "wide"))

    def run(points, scales, frequencies, *others):
        return jax.shard_map(
            functools.partial(on_device, frequencies.shape[1]),
            mesh=mesh,
            in_specs=in_specs,
            out_specs=out_specs,
            check_vma=False,
        )(points, scales, frequencies, *others)

    return run
```

```python
import functools
import math
from typing import NamedTuple

import jax
import jax.numpy as jnp
from jax import lax
from jax.experimental import pallas as pl
from jax.experimental.pallas import tpu as pltpu
from jax.sharding import PartitionSpec as P

GROUP = 128
BLOCKS = 2
NOISE_VAR = 0.1
LN2 = math.log(2.0)
TO_TURNS = 1.0 / (2.0 * math.pi)
TO_U = math.sqrt(5.0) / LN2
SINE = (-6.283164044164058, 41.33714235333657, -81.34076831835199, 70.99342806157215)
FIRST = 58
F32 = jnp.float32
BF16 = jnp.bfloat16


class Sizes(NamedTuple):
    shard: int
    share: int
    own: int
    rows: int


def thirds(x):
    high = x.astype(BF16).astype(F32)
    rest = x - high
    mid = rest.astype(BF16).astype(F32)
    low = (rest - mid).astype(BF16).astype(F32)
    return high, mid, low


def halves(x):
    high = x.astype(BF16)
    return high, (x - high.astype(F32)).astype(BF16)


def stack_rows(rows):
    width = max(row.shape[1] for row in rows)
    at = lax.broadcasted_iota(jnp.int32, (8, width), 0)
    out = jnp.zeros((8, width), F32)
    for index, row in enumerate(rows):
        out = jnp.where(at == index, row, out)
    return out


def left_terms(parts, extra):
    high, mid, low = parts
    return jnp.concatenate([high, high, mid, mid, high, low, extra, jnp.zeros_like(high)], 0)


def right_terms(parts, extra):
    high, mid, low = parts
    return jnp.concatenate([high, mid, high, mid, low, high, extra, jnp.zeros_like(high)], 0)


def cosine(turns):
    fraction = turns - jnp.round(turns)
    shifted = jnp.abs(fraction) - 0.25
    square = shifted * shifted
    value = SINE[-1]
    for factor in SINE[-2::-1]:
        value = value * square + factor
    return value * shifted


def group_cut(inside):
    return pl.ds(pl.multiple_of(inside * GROUP, GROUP), GROUP)


def group_of(ref, index):
    return ref[:, pl.ds(pl.multiple_of(index * GROUP, GROUP), GROUP)]


def dots(terms, high, low, samples):
    both = jnp.dot(terms, high, preferred_element_type=F32)
    return both[:samples] + both[samples:] + jnp.dot(terms[:samples], low, preferred_element_type=F32)


def two_parts(x):
    high, low = halves(x)
    return jnp.concatenate([high, low], 0)


def core_of(side):
    core = lax.rem(lax.axis_index("wide"), 2)
    return core if side else 1 - core


class Block(NamedTuple):
    block: int
    side: int
    begin: int
    count: int

    def at(self, sizes, table, k):
        narrow = lax.axis_index("narrow")
        entry = narrow * sizes.share + core_of(self.side) * (sizes.share // 2) + self.begin + k
        return table[self.block, entry] - narrow * sizes.shard


class Other(NamedTuple):
    begin: int
    count: int

    def at(self, sizes, table, k):
        return table[self.begin + k]


class Natural(NamedTuple):
    side: int
    begin: int
    count: int

    def at(self, sizes, table, k):
        part = self.begin + k // sizes.own
        return (2 * part + core_of(self.side)) * sizes.own + k % sizes.own


def row_group(sizes, table, block, j):
    group = table[block, lax.axis_index("wide") * sizes.rows + j]
    return group // sizes.shard, lax.rem(group, sizes.shard)


def call(body, name, shapes, tables, arrays, flops, after=(), scratch=(), kinds=None, limit=6):
    kinds = kinds or [pltpu.VMEM] * len(arrays)
    spaces = [pltpu.SMEM] * len(tables) + kinds + [pl.ANY] * len(after)

    def run(*refs):
        inputs = len(tables) + len(arrays)
        body(*refs[:inputs], *refs[inputs + len(after) :])

    return pl.pallas_call(
        run,
        out_shape=[jax.ShapeDtypeStruct(*shape) for shape in shapes],
        in_specs=[pl.BlockSpec(memory_space=space) for space in spaces],
        out_specs=[pl.BlockSpec(memory_space=pltpu.VMEM)] * len(shapes),
        scratch_shapes=list(scratch),
        compiler_params=pltpu.CompilerParams(vmem_limit_bytes=limit << 20),
        cost_estimate=pl.CostEstimate(flops=int(flops), bytes_accessed=0, transcendentals=0),
        name=name,
    )(*tables, *arrays, *after)


def loop(count, body, start=None):
    if count == 1:
        return body(0, start)
    return lax.fori_loop(0, count, body, start)


def prior_tiles(sizes, which, factor, table, left, fw, points, targets, noise, out):
    features, width = left.shape[0], out.shape[1]
    tile, chunk = math.gcd(width, 512), math.gcd(features, 2048)
    per = tile // GROUP
    ones = jnp.ones((1, tile), F32)

    def one_tile(at, _):
        groups = [which.at(sizes, table, at * per + k) for k in range(per)]
        coords = jnp.concatenate([group_of(points, group) for group in groups], 1)
        right = right_terms(thirds(coords), stack_rows([ones] * 3)).astype(BF16)

        def one_chunk(index, total):
            cut = pl.ds(pl.multiple_of(index * chunk, chunk), chunk)
            turns = jnp.dot(left[cut, :], right, preferred_element_type=F32)
            values = cosine(turns).astype(BF16)
            return total + jnp.dot(fw[:, cut], values, preferred_element_type=F32)

        total = loop(features // chunk, one_chunk, jnp.zeros((out.shape[0], tile), F32))
        out[:, pl.ds(pl.multiple_of(at * tile, tile), tile)] = -factor * total
        for k, group in enumerate(groups):

            @pl.when(group // sizes.own == lax.axis_index("wide"))
            def _():
                inside = lax.rem(group, sizes.own)
                out[:, group_cut(at * per + k)] += group_of(targets, inside) - group_of(noise, inside)

        return 0

    loop(width // tile, one_tile, 0)


def first_body(sizes, which, factor, table, *refs):
    sources, (out, left, picked), held, sems = refs[:6], refs[6:9], refs[9:15], refs[15]
    copies = [
        pltpu.make_async_copy(source, target, sems.at[index])
        for index, (source, target) in enumerate(zip(sources, held))
    ]
    for copy in copies:
        copy.start()
    freq, phase, points, fw, targets, noise = held
    copies[0].wait()
    copies[1].wait()
    features = freq.shape[1]
    step = math.gcd(features, 1024)

    def one_step(index, _):
        cut = pl.ds(pl.multiple_of(index * step, step), step)
        extra = stack_rows(thirds(phase[:, cut] * TO_TURNS))
        terms = left_terms(thirds(freq[:, cut] * TO_TURNS), extra)
        left[cut, :] = terms.T.astype(BF16)
        return 0

    loop(features // step, one_step, 0)
    copies[2].wait()
    for block in range(BLOCKS):
        for j in range(sizes.rows):
            owner, inside = row_group(sizes, table, block, j)
            mine = jnp.where(owner == lax.axis_index("narrow"), 1.0, 0.0)
            picked[block, :, j * GROUP : (j + 1) * GROUP] = group_of(points, inside) * mine
    for copy in copies[3:]:
        copy.wait()
    prior_tiles(sizes, which, factor, table, left, fw, points, targets, noise, out)


def prior_first(sizes, which, factor, table, arrays):
    freq, fw = arrays[0], arrays[3]
    samples, features = fw.shape
    width = which.count * GROUP
    shapes = [
        ((samples, width), F32),
        ((features, 64), BF16),
        ((BLOCKS, freq.shape[0], sizes.rows * GROUP), F32),
    ]
    scratch = [pltpu.VMEM(array.shape, array.dtype) for array in arrays]
    return call(
        functools.partial(first_body, sizes, which, factor),
        "prior_first",
        shapes,
        (table,),
        arrays,
        2300 * features * width,
        scratch=[*scratch, pltpu.SemaphoreType.DMA((len(arrays),))],
        kinds=[pltpu.HBM] * len(arrays),
        limit=FIRST,
    )


def prior_part(sizes, which, factor, table, arrays, name, after=(), cost=800):
    (samples, features), width = arrays[1].shape, which.count * GROUP
    return call(
        functools.partial(prior_tiles, sizes, which, factor),
        name,
        [((samples, width), F32)],
        (table,),
        arrays,
        cost * features * width,
        after,
        limit=14,
    )[0]


def inverse_body(block, side, x, inverses, *refs):
    *before, out = refs
    samples, depth = x.shape
    rows = out.shape[1]
    tile = math.gcd(rows, 512)
    span = pl.ds(pl.multiple_of(core_of(side) * depth, depth), depth)
    high, low = halves(x[...])
    turned = jnp.concatenate([high.astype(F32), low.astype(F32)], 0).T.astype(BF16)
    for row in range(0, rows, tile):
        cut = slice(row, row + tile)
        high, low = halves(inverses[block, cut, span])
        total = jnp.dot(high, turned, preferred_element_type=F32)
        total += jnp.dot(low, turned, preferred_element_type=F32)
        total = total.T
        total = total[:samples] + total[samples:]
        out[:, cut] = total + before[0][:, cut] if before else total


def inverse_part(x, inverses, block, side, before, name):
    rows, depth = inverses.shape[1], x.shape[1]
    return call(
        functools.partial(inverse_body, block, side),
        name,
        [((x.shape[0], rows), F32)],
        (),
        (x, inverses, *before),
        512 * depth * rows,
    )[0]


def add_body(count, *refs):
    terms, outs = refs[: 2 * count], refs[2 * count :]
    rows = [terms[k][...] + terms[count + k][...] for k in range(count)]
    if len(rows) == len(outs):
        for out, row in zip(outs, rows):
            out[...] = row
    elif len(rows) == 1:
        middle = rows[0].shape[0] // 2
        outs[0][...] = rows[0][:middle]
        outs[1][...] = rows[0][middle:]
    else:
        middle = rows[0].shape[0]
        outs[0][:middle] = rows[0]
        outs[0][middle:] = rows[1]


def add(left, right, outs, after, name):
    rows = sum(array.shape[0] for array in left) // outs
    shapes = [((rows, left[0].shape[1]), F32)] * outs
    return call(
        functools.partial(add_body, len(left)), name, shapes, (), (*left, *right), 1e8, after
    )


def kernel_coords(coords, scales):
    centred = (coords - 0.5) * (scales * TO_U)
    return centred, jnp.sum(centred * centred, axis=0, keepdims=True)


def lefts_body(rows, scales, out):
    for block in range(rows.shape[0]):
        for begin in range(0, rows.shape[2], GROUP):
            cut = slice(begin, begin + GROUP)
            centred, norm = kernel_coords(rows[block, :, cut], scales[...])
            ones = jnp.ones((1, GROUP), F32)
            extra = stack_rows([*thirds(norm), ones, ones, ones])
            matrix = left_terms([-2.0 * part for part in thirds(centred)], extra)
            out[block, cut, :] = matrix.T.astype(BF16)


def lefts_part(rows, scales, after):
    shape = (rows.shape[0], rows.shape[2], 64)
    return call(lefts_body, "lefts", [(shape, BF16)], (), (rows, scales), 1e8, after)[0]


def tiles_of(left, right):
    square = jnp.maximum(jnp.dot(left, right, preferred_element_type=F32), 1e-20)
    u = square * lax.rsqrt(square)
    values = (1.0 + u * (LN2 + (LN2 * LN2 / 3.0) * u)) * jnp.exp2(-u)
    return halves(values)


def right_of(sizes, which, table, points, scales, at, per):
    groups = [which.at(sizes, table, at * per + k) for k in range(per)]
    coords = jnp.concatenate([group_of(points, group) for group in groups], 1)
    centred, norm = kernel_coords(coords, scales[...])
    ones = jnp.ones((1, per * GROUP), F32)
    extra = stack_rows([ones, ones, ones, *thirds(norm)])
    return right_terms(thirds(centred), extra).astype(BF16)


def tiles_body(sizes, which, block, table, lefts, points, scales, high_out, low_out):
    depth, width = high_out.shape
    tile = math.gcd(width, 512)

    def one_tile(at, _):
        right = right_of(sizes, which, table, points, scales, at, tile // GROUP)
        here = pl.ds(pl.multiple_of(at * tile, tile), tile)
        high_out[:, here], low_out[:, here] = tiles_of(lefts[block], right)
        return 0

    loop(width // tile, one_tile, 0)


def tiles_part(sizes, which, block, table, lefts, points, scales, name, after=()):
    depth, width = lefts.shape[1], which.count * GROUP
    return call(
        functools.partial(tiles_body, sizes, which, block),
        name,
        [((depth, width), BF16)] * 2,
        (table,),
        (lefts, points, scales),
        300 * depth * width,
        after,
        limit=10,
    )


def product_body(update, high, low, carry, out):
    samples, width = carry.shape
    terms = two_parts(update[...])
    tile = math.gcd(width, 256)
    for begin in range(0, width, tile):
        cut = slice(begin, begin + tile)
        out[:, cut] = carry[:, cut] - dots(terms, high[:, cut], low[:, cut], samples)


def product_part(update, tiles, carry, name):
    flops = 384 * update.shape[1] * carry.shape[1]
    arrays = (update, *tiles, carry)
    return call(product_body, name, [(carry.shape, F32)], (), arrays, flops)[0]


def fused_body(sizes, which, table, lefts, points, scales, update, carry, out):
    samples, width = carry.shape
    terms = two_parts(update[...])
    tile = math.gcd(width, 512)

    def one_tile(at, _):
        right = right_of(sizes, which, table, points, scales, at, tile // GROUP)
        here = pl.ds(pl.multiple_of(at * tile, tile), tile)
        out[:, here] = carry[:, here] - dots(terms, *tiles_of(lefts[0], right), samples)
        return 0

    loop(width // tile, one_tile, 0)


def fused_part(sizes, which, table, lefts, points, scales, update, carry, name, after=()):
    return call(
        functools.partial(fused_body, sizes, which),
        name,
        [(carry.shape, F32)],
        (table,),
        (lefts, points, scales, update, carry),
        1600 * lefts.shape[1] * carry.shape[1],
        after,
        limit=12,
    )[0]


def arrange_body(sizes, layout, table, others, update, *refs):
    *pieces, out = refs
    for which, piece in zip(layout, pieces):
        source = others if isinstance(which, Other) else table
        for k in range(which.count):
            group = which.at(sizes, source, k)
            cut = group_cut(lax.rem(group, sizes.own))
            out[group // sizes.own, :, cut] = piece[:, k * GROUP : (k + 1) * GROUP]
    for j in range(sizes.rows):
        owner, inside = row_group(sizes, table, 0, j)

        @pl.when(owner == lax.axis_index("narrow"))
        def _():
            cut = group_cut(lax.rem(inside, sizes.own))
            diagonal = update[:, j * GROUP : (j + 1) * GROUP]
            out[inside // sizes.own, :, cut] -= NOISE_VAR * diagonal


def arrange_part(sizes, layout, table, others, update, pieces, after):
    shape = (sizes.shard // sizes.own, update.shape[0], sizes.own * GROUP)
    return call(
        functools.partial(arrange_body, sizes, layout),
        "arrange",
        [(shape, F32)],
        (table, others),
        (update, *pieces),
        1e8,
        after,
    )[0]


def last_body(sizes, side, table, update, arranged, *refs):
    *tiles, out = refs
    samples = update.shape[0]
    terms = two_parts(update[...])
    core = core_of(side)
    width = sizes.own * GROUP
    tile = math.gcd(width, 256)
    each = out.shape[0] * 2 // len(tiles)
    for part in range(out.shape[0]):
        high, low = tiles[2 * (part // each)], tiles[2 * (part // each) + 1]
        for begin in range(0, width, tile):
            base = (part % each) * width + begin
            cut, here = slice(base, base + tile), slice(begin, begin + tile)
            value = dots(terms, high[:, cut], low[:, cut], samples)
            out[part, :, here] = arranged[2 * part + core, :, here] - value
    for j in range(sizes.rows):
        owner, inside = row_group(sizes, table, 1, j)
        part = inside // sizes.own

        @pl.when((owner == lax.axis_index("narrow")) & (lax.rem(part, 2) == core))
        def _():
            cut = group_cut(lax.rem(inside, sizes.own))
            out[part // 2, :, cut] -= NOISE_VAR * update[:, j * GROUP : (j + 1) * GROUP]


def last_part(sizes, side, table, update, arranged, tiles, name):
    parts, samples, width = arranged.shape
    return call(
        functools.partial(last_body, sizes, side),
        name,
        [((parts // 2, samples, width), F32)],
        (table,),
        (update, arranged, *tiles),
        384 * update.shape[1] * parts * width // 2,
    )[0]


def exchange(value, axis, mask):
    count = lax.axis_size(axis)
    return lax.ppermute(value, axis, [(i, i ^ mask) for i in range(count)])


def butterfly(pair, axis, masks, windows, name):
    steps = list(zip(masks, masks[1:] + masks[:1]))
    for index, (one, two) in enumerate(steps):
        got = exchange(pair[0], axis, one), exchange(pair[1], axis, two)
        beside = windows[index](pair[0]) if index < len(windows) else []
        last = index == len(steps) - 1
        pair = add(pair, got, 1 if last else 2, beside, f"{name}_{index}")
    return pair[0]


def sum_wide(theirs, mine, windows, name):
    count = lax.axis_size("wide")
    pair = add((mine,), (exchange(theirs, "wide", 1),), 2, (), f"{name}_core")
    masks = [1 << bit for bit in range(1, count.bit_length() - 1)]
    return butterfly(pair, "wide", masks, windows, name)


def narrow_masks():
    return [(2 << bit) - 1 for bit in range(lax.axis_size("narrow").bit_length() - 1)]


def sum_narrow(value, windows, name):
    rows = value.shape[0] // 2
    return butterfly((value[:rows], value[rows:]), "narrow", narrow_masks(), windows, name)


def pick_body(mine, got, *outs):
    chip = lax.axis_index("wide") // 2
    for mask, out in enumerate(outs):
        out[...] = mine[chip ^ mask] + got[chip ^ mask]


def scatter_wide(theirs, mine):
    parts, *shape = mine.shape
    got = exchange(theirs, "wide", 1)
    shapes = [(tuple(shape), F32)] * parts
    own, *sent = call(pick_body, "pick", shapes, (), (mine, got), 1e8)
    return sum((exchange(part, "wide", 2 * mask) for mask, part in enumerate(sent, 1)), own)


def other_groups(table, sizes):
    narrow = lax.axis_index("narrow")
    used = lax.dynamic_slice_in_dim(table, narrow * sizes.share, sizes.share, 1).reshape(-1)
    used = used - narrow * sizes.shard
    ids = jnp.arange(sizes.shard, dtype=jnp.int32)
    free = ~jnp.any(ids[:, None] == used[None, :], axis=1)
    before = (ids[None, :] < ids[:, None]) & free[None, :]
    spot = jnp.sum(before.astype(jnp.int32), axis=1)
    slots = jnp.arange(sizes.shard - BLOCKS * sizes.share, dtype=jnp.int32)
    hit = (spot[None, :] == slots[:, None]) & free[None, :]
    return jnp.sum(jnp.where(hit, ids[None, :], 0), axis=1).astype(jnp.int32)


def on_device(
    all_features,
    points,
    scales,
    frequencies,
    phases,
    feature_weights,
    targets,
    noise,
    inverses,
    groups,
):
    wide_count, narrow_count = lax.axis_size("wide"), lax.axis_size("narrow")
    shard_groups = points.shape[1] // GROUP
    sizes = Sizes(
        shard_groups,
        groups.shape[1] // narrow_count,
        shard_groups // wide_count,
        groups.shape[1] // wide_count,
    )
    half = sizes.share // 2
    factor = math.sqrt(2.0 / all_features)
    targets, phases, scales = targets[None, :], phases[None, :], scales[:, None]
    left_over = sizes.shard - BLOCKS * sizes.share
    others = other_groups(groups, sizes) if left_over else groups

    arrays = (frequencies, phases, points, feature_weights, targets, noise)
    halves_0 = [Block(0, side, 0, half) for side in range(2)]
    halves_1 = [Block(1, side, 0, half) for side in range(2)]
    first_theirs, left, picked = prior_first(sizes, halves_0[0], factor, groups, arrays)
    shared = (left, feature_weights, points, targets, noise)
    first_mine = prior_part(
        sizes, halves_0[1], factor, groups, shared, "prior_mine", cost=2300
    )
    flat = picked.reshape(-1, picked.shape[2])

    def row_step(index, after):
        got = exchange(row_sums[-1], "narrow", narrow_masks()[index])
        row_sums.extend(add((row_sums[-1],), (got,), 1, (after,), f"rows_{index}"))

    row_sums = [flat]
    row_step(0, first_mine)

    piece = math.gcd(half, 4)
    pieces = [Block(1, side, begin, piece) for side in range(2) for begin in range(0, half, piece)]
    later = {}

    def prior_beside(chosen, extra, cost):
        def run(after):
            made = []
            for which in chosen:
                name = f"prior_{which.side}_{which.begin}"
                later[which] = prior_part(
                    sizes, which, factor, groups, shared, name, (after,), cost
                )
                made.append(later[which])
            return made + extra(after, made)

        return run

    def weights(mine, block, windows):
        theirs = exchange(mine, "wide", 1)
        part = inverse_part(mine, inverses, block, 1, (), f"inverse_{block}_mine")
        part = inverse_part(theirs, inverses, block, 0, (part,), f"inverse_{block}_theirs")
        return sum_narrow(part, windows, f"narrow_{block}")

    shares = [pieces[k::4] if len(pieces) > 4 else pieces[k : k + 1] for k in range(4)]
    lefts, tiles_0 = [], []

    def rows_beside(after, made):
        for index in range(1, len(narrow_masks())):
            row_step(index, made[-1])
        return row_sums[-1:]

    def lefts_beside(after, made):
        lefts.append(lefts_part(row_sums[-1].reshape(picked.shape), scales, (made[-1],)))
        return lefts

    def tiles_0_beside(side):
        def run(after, made):
            name = f"tiles_0_{side}"
            tiles_0.append(
                tiles_part(
                    sizes, halves_1[side], 0, groups, lefts[0], points, scales, name, (after,)
                )
            )
            return list(tiles_0[-1])

        return run

    extras = [rows_beside, lefts_beside, tiles_0_beside(0), tiles_0_beside(1)]
    costs = [2300, 2300, 400, 400]
    beside = [prior_beside(*terms) for terms in zip(shares, extras, costs)]
    whole = sum_wide(first_theirs, first_mine, beside[:2], "wide_0")
    update = weights(whole, 0, beside[2:])
    carries = [
        jnp.concatenate([later[which] for which in pieces if which.side == side], 1)
        for side in range(2)
    ]
    rest = [Other(begin, piece) for begin in range(0, left_over, piece)]
    rest_prior = [
        prior_part(sizes, which, factor, others, shared, f"prior_rest_{which.begin}")
        for which in rest
    ]
    tiles = functools.partial(tiles_part, sizes, lefts=lefts[0], points=points, scales=scales)
    fused = functools.partial(
        fused_part, sizes, lefts=lefts[0], points=points, scales=scales, update=update
    )
    following = [
        product_part(update, tiles_0[side], carries[side], f"product_0_{side}") for side in range(2)
    ]
    own_pieces = []

    def own_beside(side, carry):
        def run(after):
            name = f"fused_{side}"
            made = fused(halves_0[side], table=groups, carry=carry, name=name, after=(after,))
            own_pieces.append(made)
            return [made]

        return run

    windows = [own_beside(0, first_theirs), own_beside(1, first_mine)]
    whole = sum_wide(*following, windows, "wide_1")
    rest_pieces = [
        fused(which, table=others, carry=carry, name=f"fused_rest_{which.begin}")
        for which, carry in zip(rest, rest_prior)
    ]
    each = max(1, 8 // sizes.own)
    ahead = [[], []]
    arranged = []

    def ahead_beside(side):
        def run(after):
            for begin in range(0, wide_count // 2, each):
                ahead[side] += tiles(
                    Natural(side, begin, each * sizes.own),
                    block=1,
                    table=groups,
                    name=f"tiles_1_{side}_{begin}",
                    after=(after,),
                )
            made = list(ahead[side])
            if side:
                layout = [*halves_0, *halves_1, *rest]
                parts = [*own_pieces, *following, *rest_pieces]
                arranged.append(
                    arrange_part(sizes, layout, groups, others, update, parts, (after,))
                )
                made += arranged
            return made

        return run

    update_1 = weights(whole, 1, [ahead_beside(0), ahead_beside(1)])
    theirs, mine = (
        last_part(sizes, side, groups, update_1, arranged[0], ahead[side], f"last_{side}")
        for side in range(2)
    )
    return scatter_wide(theirs, mine), jnp.stack([update, update_1])


def solution(mesh):
    in_specs = (
        P(None, "narrow"),
        P(),
        P(None, "wide"),
        P("wide"),
        P(None, "wide"),
        P(("narrow", "wide")),
        P(None, ("narrow", "wide")),
        P(None, "wide", "narrow"),
        P(),
    )
    out_specs = (P(None, ("narrow", "wide")), P(None, None, "wide"))

    def run(points, scales, frequencies, *others):
        return jax.shard_map(
            functools.partial(on_device, frequencies.shape[1]),
            mesh=mesh,
            in_specs=in_specs,
            out_specs=out_specs,
            check_vma=False,
        )(points, scales, frequencies, *others)

    return run
```

```python
import functools
import math
from typing import NamedTuple

import jax
import jax.numpy as jnp
from jax import lax
from jax.experimental import pallas as pl
from jax.experimental.pallas import tpu as pltpu
from jax.sharding import PartitionSpec as P

GROUP = 128
BLOCKS = 2
NOISE_VAR = 0.1
LN2 = math.log(2.0)
TO_TURNS = 1.0 / (2.0 * math.pi)
TO_U = math.sqrt(5.0) / LN2
SINE = (-6.283164044164058, 41.33714235333657, -81.34076831835199, 70.99342806157215)
FIRST = 58
F32 = jnp.float32
BF16 = jnp.bfloat16


class Sizes(NamedTuple):
    shard: int
    share: int
    own: int
    rows: int


def thirds(x):
    high = x.astype(BF16).astype(F32)
    rest = x - high
    mid = rest.astype(BF16).astype(F32)
    low = (rest - mid).astype(BF16).astype(F32)
    return high, mid, low


def halves(x):
    high = x.astype(BF16)
    return high, (x - high.astype(F32)).astype(BF16)


def stack_rows(rows):
    width = max(row.shape[1] for row in rows)
    at = lax.broadcasted_iota(jnp.int32, (8, width), 0)
    out = jnp.zeros((8, width), F32)
    for index, row in enumerate(rows):
        out = jnp.where(at == index, row, out)
    return out


def left_terms(parts, extra):
    high, mid, low = parts
    return jnp.concatenate([high, high, mid, mid, high, low, extra, jnp.zeros_like(high)], 0)


def right_terms(parts, extra):
    high, mid, low = parts
    return jnp.concatenate([high, mid, high, mid, low, high, extra, jnp.zeros_like(high)], 0)


def cosine(turns):
    fraction = turns - jnp.round(turns)
    shifted = jnp.abs(fraction) - 0.25
    square = shifted * shifted
    value = SINE[-1]
    for factor in SINE[-2::-1]:
        value = value * square + factor
    return value * shifted


def group_cut(inside):
    return pl.ds(pl.multiple_of(inside * GROUP, GROUP), GROUP)


def group_of(ref, index):
    return ref[:, pl.ds(pl.multiple_of(index * GROUP, GROUP), GROUP)]


def dots(terms, high, low, samples):
    both = jnp.dot(terms, high, preferred_element_type=F32)
    return both[:samples] + both[samples:] + jnp.dot(terms[:samples], low, preferred_element_type=F32)


def two_parts(x):
    high, low = halves(x)
    return jnp.concatenate([high, low], 0)


def core_of(side):
    core = lax.rem(lax.axis_index("wide"), 2)
    return core if side else 1 - core


class Block(NamedTuple):
    block: int
    side: int
    begin: int
    count: int

    def at(self, sizes, table, k):
        narrow = lax.axis_index("narrow")
        entry = narrow * sizes.share + core_of(self.side) * (sizes.share // 2) + self.begin + k
        return table[self.block, entry] - narrow * sizes.shard


class Other(NamedTuple):
    begin: int
    count: int

    def at(self, sizes, table, k):
        return table[self.begin + k]


class Natural(NamedTuple):
    side: int
    begin: int
    count: int

    def at(self, sizes, table, k):
        part = self.begin + k // sizes.own
        return (2 * part + core_of(self.side)) * sizes.own + k % sizes.own


def row_group(sizes, table, block, j):
    group = table[block, lax.axis_index("wide") * sizes.rows + j]
    return group // sizes.shard, lax.rem(group, sizes.shard)


def call(body, name, shapes, tables, arrays, flops, after=(), scratch=(), kinds=None, limit=6):
    kinds = kinds or [pltpu.VMEM] * len(arrays)
    spaces = [pltpu.SMEM] * len(tables) + kinds + [pl.ANY] * len(after)

    def run(*refs):
        inputs = len(tables) + len(arrays)
        body(*refs[:inputs], *refs[inputs + len(after) :])

    return pl.pallas_call(
        run,
        out_shape=[jax.ShapeDtypeStruct(*shape) for shape in shapes],
        in_specs=[pl.BlockSpec(memory_space=space) for space in spaces],
        out_specs=[pl.BlockSpec(memory_space=pltpu.VMEM)] * len(shapes),
        scratch_shapes=list(scratch),
        compiler_params=pltpu.CompilerParams(vmem_limit_bytes=limit << 20),
        cost_estimate=pl.CostEstimate(flops=int(flops), bytes_accessed=0, transcendentals=0),
        name=name,
    )(*tables, *arrays, *after)


def loop(count, body, start=None):
    if count == 1:
        return body(0, start)
    return lax.fori_loop(0, count, body, start)


def prior_tiles(sizes, which, factor, table, left, fw, points, targets, noise, out):
    chunk, width = left.shape[0], out.shape[1]
    tile = math.gcd(width, 512)
    per = tile // GROUP
    ones = jnp.ones((1, tile), F32)

    def one_tile(at, _):
        groups = [which.at(sizes, table, at * per + k) for k in range(per)]
        coords = jnp.concatenate([group_of(points, group) for group in groups], 1)
        right = right_terms(thirds(coords), stack_rows([ones] * 3))

        def one_chunk(index, total):
            cut = pl.ds(pl.multiple_of(index * chunk, chunk), chunk)
            sides = [jnp.where(index == side, right, 0.0) for side in range(2)]
            both = jnp.concatenate(sides, 0).astype(BF16)
            turns = jnp.dot(left[...], both, preferred_element_type=F32)
            values = cosine(turns).astype(BF16)
            return total + jnp.dot(fw[:, cut], values, preferred_element_type=F32)

        total = loop(2, one_chunk, jnp.zeros((out.shape[0], tile), F32))
        out[:, pl.ds(pl.multiple_of(at * tile, tile), tile)] = -factor * total
        for k, group in enumerate(groups):

            @pl.when(group // sizes.own == lax.axis_index("wide"))
            def _():
                inside = lax.rem(group, sizes.own)
                out[:, group_cut(at * per + k)] += group_of(targets, inside) - group_of(noise, inside)

        return 0

    loop(width // tile, one_tile, 0)


def first_body(sizes, which, factor, table, *refs):
    sources, (out, left, picked), held, sems = refs[:6], refs[6:9], refs[9:15], refs[15]
    copies = [
        pltpu.make_async_copy(source, target, sems.at[index])
        for index, (source, target) in enumerate(zip(sources, held))
    ]
    for copy in copies:
        copy.start()
    freq, phase, points, fw, targets, noise = held
    copies[0].wait()
    copies[1].wait()
    features = freq.shape[1]
    middle = features // 2
    step = math.gcd(middle, 512)

    def one_step(index, _):
        sides = []
        for begin in (0, middle):
            cut = pl.ds(pl.multiple_of(begin + index * step, step), step)
            extra = stack_rows(thirds(phase[:, cut] * TO_TURNS))
            sides.append(left_terms(thirds(freq[:, cut] * TO_TURNS), extra))
        cut = pl.ds(pl.multiple_of(index * step, step), step)
        left[cut, :] = jnp.concatenate(sides, 0).T.astype(BF16)
        return 0

    loop(middle // step, one_step, 0)
    copies[2].wait()
    for block in range(BLOCKS):
        for j in range(sizes.rows):
            owner, inside = row_group(sizes, table, block, j)
            mine = jnp.where(owner == lax.axis_index("narrow"), 1.0, 0.0)
            picked[block, :, j * GROUP : (j + 1) * GROUP] = group_of(points, inside) * mine
    for copy in copies[3:]:
        copy.wait()
    prior_tiles(sizes, which, factor, table, left, fw, points, targets, noise, out)


def prior_first(sizes, which, factor, table, arrays):
    freq, fw = arrays[0], arrays[3]
    samples, features = fw.shape
    width = which.count * GROUP
    shapes = [
        ((samples, width), F32),
        ((features // 2, 128), BF16),
        ((BLOCKS, freq.shape[0], sizes.rows * GROUP), F32),
    ]
    scratch = [pltpu.VMEM(array.shape, array.dtype) for array in arrays]
    return call(
        functools.partial(first_body, sizes, which, factor),
        "prior_first",
        shapes,
        (table,),
        arrays,
        2300 * features * width,
        scratch=[*scratch, pltpu.SemaphoreType.DMA((len(arrays),))],
        kinds=[pltpu.HBM] * len(arrays),
        limit=FIRST,
    )


def prior_part(sizes, which, factor, table, arrays, name, after=(), cost=800):
    (samples, features), width = arrays[1].shape, which.count * GROUP
    return call(
        functools.partial(prior_tiles, sizes, which, factor),
        name,
        [((samples, width), F32)],
        (table,),
        arrays,
        cost * features * width,
        after,
        limit=14,
    )[0]


def inverse_body(block, side, x, inverses, *refs):
    *before, out = refs
    samples, depth = x.shape
    rows = out.shape[1]
    tile = math.gcd(rows, 512)
    span = pl.ds(pl.multiple_of(core_of(side) * depth, depth), depth)
    high, low = halves(x[...])
    turned = jnp.concatenate([high.astype(F32), low.astype(F32)], 0).T.astype(BF16)
    for row in range(0, rows, tile):
        cut = slice(row, row + tile)
        high, low = halves(inverses[block, cut, span])
        total = jnp.dot(high, turned, preferred_element_type=F32)
        total += jnp.dot(low, turned, preferred_element_type=F32)
        total = total.T
        total = total[:samples] + total[samples:]
        out[:, cut] = total + before[0][:, cut] if before else total


def inverse_part(x, inverses, block, side, before, name):
    rows, depth = inverses.shape[1], x.shape[1]
    return call(
        functools.partial(inverse_body, block, side),
        name,
        [((x.shape[0], rows), F32)],
        (),
        (x, inverses, *before),
        512 * depth * rows,
    )[0]


def add_body(count, *refs):
    terms, outs = refs[: 2 * count], refs[2 * count :]
    rows = [terms[k][...] + terms[count + k][...] for k in range(count)]
    if len(rows) == len(outs):
        for out, row in zip(outs, rows):
            out[...] = row
    elif len(rows) == 1:
        middle = rows[0].shape[0] // 2
        outs[0][...] = rows[0][:middle]
        outs[1][...] = rows[0][middle:]
    else:
        middle = rows[0].shape[0]
        outs[0][:middle] = rows[0]
        outs[0][middle:] = rows[1]


def add(left, right, outs, after, name):
    rows = sum(array.shape[0] for array in left) // outs
    shapes = [((rows, left[0].shape[1]), F32)] * outs
    return call(
        functools.partial(add_body, len(left)), name, shapes, (), (*left, *right), 1e8, after
    )


def kernel_coords(coords, scales):
    centred = (coords - 0.5) * (scales * TO_U)
    return centred, jnp.sum(centred * centred, axis=0, keepdims=True)


def lefts_body(rows, scales, out):
    for block in range(rows.shape[0]):
        for begin in range(0, rows.shape[2], GROUP):
            cut = slice(begin, begin + GROUP)
            centred, norm = kernel_coords(rows[block, :, cut], scales[...])
            ones = jnp.ones((1, GROUP), F32)
            extra = stack_rows([*thirds(norm), ones, ones, ones])
            matrix = left_terms([-2.0 * part for part in thirds(centred)], extra)
            out[block, cut, :] = matrix.T.astype(BF16)


def lefts_part(rows, scales, after):
    shape = (rows.shape[0], rows.shape[2], 64)
    return call(lefts_body, "lefts", [(shape, BF16)], (), (rows, scales), 1e8, after)[0]


def tiles_of(left, right):
    square = jnp.maximum(jnp.dot(left, right, preferred_element_type=F32), 1e-20)
    u = square * lax.rsqrt(square)
    values = (1.0 + u * (LN2 + (LN2 * LN2 / 3.0) * u)) * jnp.exp2(-u)
    return halves(values)


def right_of(sizes, which, table, points, scales, at, per):
    groups = [which.at(sizes, table, at * per + k) for k in range(per)]
    coords = jnp.concatenate([group_of(points, group) for group in groups], 1)
    centred, norm = kernel_coords(coords, scales[...])
    ones = jnp.ones((1, per * GROUP), F32)
    extra = stack_rows([ones, ones, ones, *thirds(norm)])
    return right_terms(thirds(centred), extra).astype(BF16)


def tiles_body(sizes, which, block, table, lefts, points, scales, high_out, low_out):
    depth, width = high_out.shape
    tile = math.gcd(width, 512)

    def one_tile(at, _):
        right = right_of(sizes, which, table, points, scales, at, tile // GROUP)
        here = pl.ds(pl.multiple_of(at * tile, tile), tile)
        high_out[:, here], low_out[:, here] = tiles_of(lefts[block], right)
        return 0

    loop(width // tile, one_tile, 0)


def tiles_part(sizes, which, block, table, lefts, points, scales, name, after=()):
    depth, width = lefts.shape[1], which.count * GROUP
    return call(
        functools.partial(tiles_body, sizes, which, block),
        name,
        [((depth, width), BF16)] * 2,
        (table,),
        (lefts, points, scales),
        300 * depth * width,
        after,
        limit=10,
    )


def product_body(update, high, low, carry, out):
    samples, width = carry.shape
    terms = two_parts(update[...])
    tile = math.gcd(width, 256)
    for begin in range(0, width, tile):
        cut = slice(begin, begin + tile)
        out[:, cut] = carry[:, cut] - dots(terms, high[:, cut], low[:, cut], samples)


def product_part(update, tiles, carry, name):
    flops = 384 * update.shape[1] * carry.shape[1]
    arrays = (update, *tiles, carry)
    return call(product_body, name, [(carry.shape, F32)], (), arrays, flops)[0]


def fused_body(sizes, which, table, lefts, points, scales, update, carry, out):
    samples, width = carry.shape
    terms = two_parts(update[...])
    tile = math.gcd(width, 512)

    def one_tile(at, _):
        right = right_of(sizes, which, table, points, scales, at, tile // GROUP)
        here = pl.ds(pl.multiple_of(at * tile, tile), tile)
        out[:, here] = carry[:, here] - dots(terms, *tiles_of(lefts[0], right), samples)
        return 0

    loop(width // tile, one_tile, 0)


def fused_part(sizes, which, table, lefts, points, scales, update, carry, name, after=()):
    return call(
        functools.partial(fused_body, sizes, which),
        name,
        [(carry.shape, F32)],
        (table,),
        (lefts, points, scales, update, carry),
        1600 * lefts.shape[1] * carry.shape[1],
        after,
        limit=12,
    )[0]


def arrange_body(sizes, layout, table, others, update, *refs):
    *pieces, out = refs
    for which, piece in zip(layout, pieces):
        source = others if isinstance(which, Other) else table
        for k in range(which.count):
            group = which.at(sizes, source, k)
            cut = group_cut(lax.rem(group, sizes.own))
            out[group // sizes.own, :, cut] = piece[:, k * GROUP : (k + 1) * GROUP]
    for j in range(sizes.rows):
        owner, inside = row_group(sizes, table, 0, j)

        @pl.when(owner == lax.axis_index("narrow"))
        def _():
            cut = group_cut(lax.rem(inside, sizes.own))
            diagonal = update[:, j * GROUP : (j + 1) * GROUP]
            out[inside // sizes.own, :, cut] -= NOISE_VAR * diagonal


def arrange_part(sizes, layout, table, others, update, pieces, after):
    shape = (sizes.shard // sizes.own, update.shape[0], sizes.own * GROUP)
    return call(
        functools.partial(arrange_body, sizes, layout),
        "arrange",
        [(shape, F32)],
        (table, others),
        (update, *pieces),
        1e8,
        after,
    )[0]


def last_body(sizes, side, table, update, arranged, *refs):
    *tiles, out = refs
    samples = update.shape[0]
    terms = two_parts(update[...])
    core = core_of(side)
    width = sizes.own * GROUP
    tile = math.gcd(width, 256)
    each = out.shape[0] * 2 // len(tiles)
    for part in range(out.shape[0]):
        high, low = tiles[2 * (part // each)], tiles[2 * (part // each) + 1]
        for begin in range(0, width, tile):
            base = (part % each) * width + begin
            cut, here = slice(base, base + tile), slice(begin, begin + tile)
            value = dots(terms, high[:, cut], low[:, cut], samples)
            out[part, :, here] = arranged[2 * part + core, :, here] - value
    for j in range(sizes.rows):
        owner, inside = row_group(sizes, table, 1, j)
        part = inside // sizes.own

        @pl.when((owner == lax.axis_index("narrow")) & (lax.rem(part, 2) == core))
        def _():
            cut = group_cut(lax.rem(inside, sizes.own))
            out[part // 2, :, cut] -= NOISE_VAR * update[:, j * GROUP : (j + 1) * GROUP]


def last_part(sizes, side, table, update, arranged, tiles, name):
    parts, samples, width = arranged.shape
    return call(
        functools.partial(last_body, sizes, side),
        name,
        [((parts // 2, samples, width), F32)],
        (table,),
        (update, arranged, *tiles),
        384 * update.shape[1] * parts * width // 2,
    )[0]


def exchange(value, axis, mask):
    count = lax.axis_size(axis)
    return lax.ppermute(value, axis, [(i, i ^ mask) for i in range(count)])


def butterfly(pair, axis, masks, windows, name):
    steps = list(zip(masks, masks[1:] + masks[:1]))
    for index, (one, two) in enumerate(steps):
        got = exchange(pair[0], axis, one), exchange(pair[1], axis, two)
        beside = windows[index](pair[0]) if index < len(windows) else []
        last = index == len(steps) - 1
        pair = add(pair, got, 1 if last else 2, beside, f"{name}_{index}")
    return pair[0]


def sum_wide(theirs, mine, windows, name):
    count = lax.axis_size("wide")
    pair = add((mine,), (exchange(theirs, "wide", 1),), 2, (), f"{name}_core")
    masks = [1 << bit for bit in range(1, count.bit_length() - 1)]
    return butterfly(pair, "wide", masks, windows, name)


def narrow_masks():
    return [(2 << bit) - 1 for bit in range(lax.axis_size("narrow").bit_length() - 1)]


def sum_narrow(value, windows, name):
    rows = value.shape[0] // 2
    return butterfly((value[:rows], value[rows:]), "narrow", narrow_masks(), windows, name)


def pick_body(mine, got, *outs):
    chip = lax.axis_index("wide") // 2
    for mask, out in enumerate(outs):
        out[...] = mine[chip ^ mask] + got[chip ^ mask]


def scatter_wide(theirs, mine):
    parts, *shape = mine.shape
    got = exchange(theirs, "wide", 1)
    shapes = [(tuple(shape), F32)] * parts
    own, *sent = call(pick_body, "pick", shapes, (), (mine, got), 1e8)
    return sum((exchange(part, "wide", 2 * mask) for mask, part in enumerate(sent, 1)), own)


def other_groups(table, sizes):
    narrow = lax.axis_index("narrow")
    used = lax.dynamic_slice_in_dim(table, narrow * sizes.share, sizes.share, 1).reshape(-1)
    used = used - narrow * sizes.shard
    ids = jnp.arange(sizes.shard, dtype=jnp.int32)
    free = ~jnp.any(ids[:, None] == used[None, :], axis=1)
    before = (ids[None, :] < ids[:, None]) & free[None, :]
    spot = jnp.sum(before.astype(jnp.int32), axis=1)
    slots = jnp.arange(sizes.shard - BLOCKS * sizes.share, dtype=jnp.int32)
    hit = (spot[None, :] == slots[:, None]) & free[None, :]
    return jnp.sum(jnp.where(hit, ids[None, :], 0), axis=1).astype(jnp.int32)


def on_device(
    all_features,
    points,
    scales,
    frequencies,
    phases,
    feature_weights,
    targets,
    noise,
    inverses,
    groups,
):
    wide_count, narrow_count = lax.axis_size("wide"), lax.axis_size("narrow")
    shard_groups = points.shape[1] // GROUP
    sizes = Sizes(
        shard_groups,
        groups.shape[1] // narrow_count,
        shard_groups // wide_count,
        groups.shape[1] // wide_count,
    )
    half = sizes.share // 2
    factor = math.sqrt(2.0 / all_features)
    targets, phases, scales = targets[None, :], phases[None, :], scales[:, None]
    left_over = sizes.shard - BLOCKS * sizes.share
    others = other_groups(groups, sizes) if left_over else groups

    arrays = (frequencies, phases, points, feature_weights, targets, noise)
    halves_0 = [Block(0, side, 0, half) for side in range(2)]
    halves_1 = [Block(1, side, 0, half) for side in range(2)]
    first_theirs, left, picked = prior_first(sizes, halves_0[0], factor, groups, arrays)
    shared = (left, feature_weights, points, targets, noise)
    first_mine = prior_part(
        sizes, halves_0[1], factor, groups, shared, "prior_mine", cost=2300
    )
    flat = picked.reshape(-1, picked.shape[2])

    def row_step(index, after):
        got = exchange(row_sums[-1], "narrow", narrow_masks()[index])
        row_sums.extend(add((row_sums[-1],), (got,), 1, (after,), f"rows_{index}"))

    row_sums = [flat]
    row_step(0, first_mine)

    piece = math.gcd(half, 4)
    pieces = [Block(1, side, begin, piece) for side in range(2) for begin in range(0, half, piece)]
    later = {}

    def prior_beside(chosen, extra, cost):
        def run(after):
            made = []
            for which in chosen:
                name = f"prior_{which.side}_{which.begin}"
                later[which] = prior_part(
                    sizes, which, factor, groups, shared, name, (after,), cost
                )
                made.append(later[which])
            return made + extra(after, made)

        return run

    def weights(mine, block, windows):
        theirs = exchange(mine, "wide", 1)
        part = inverse_part(mine, inverses, block, 1, (), f"inverse_{block}_mine")
        part = inverse_part(theirs, inverses, block, 0, (part,), f"inverse_{block}_theirs")
        return sum_narrow(part, windows, f"narrow_{block}")

    shares = [pieces[k::4] if len(pieces) > 4 else pieces[k : k + 1] for k in range(4)]
    lefts, tiles_0 = [], []

    def rows_beside(after, made):
        for index in range(1, len(narrow_masks())):
            row_step(index, made[-1])
        return row_sums[-1:]

    def lefts_beside(after, made):
        lefts.append(lefts_part(row_sums[-1].reshape(picked.shape), scales, (made[-1],)))
        return lefts

    def tiles_0_beside(side):
        def run(after, made):
            name = f"tiles_0_{side}"
            tiles_0.append(
                tiles_part(
                    sizes, halves_1[side], 0, groups, lefts[0], points, scales, name, (after,)
                )
            )
            return list(tiles_0[-1])

        return run

    extras = [rows_beside, lefts_beside, tiles_0_beside(0), tiles_0_beside(1)]
    costs = [2300, 2300, 400, 400]
    beside = [prior_beside(*terms) for terms in zip(shares, extras, costs)]
    whole = sum_wide(first_theirs, first_mine, beside[:2], "wide_0")
    update = weights(whole, 0, beside[2:])
    carries = [
        jnp.concatenate([later[which] for which in pieces if which.side == side], 1)
        for side in range(2)
    ]
    rest = [Other(begin, piece) for begin in range(0, left_over, piece)]
    rest_prior = [
        prior_part(sizes, which, factor, others, shared, f"prior_rest_{which.begin}")
        for which in rest
    ]
    tiles = functools.partial(tiles_part, sizes, lefts=lefts[0], points=points, scales=scales)
    fused = functools.partial(
        fused_part, sizes, lefts=lefts[0], points=points, scales=scales, update=update
    )
    following = [
        product_part(update, tiles_0[side], carries[side], f"product_0_{side}") for side in range(2)
    ]
    own_pieces = []

    def own_beside(side, carry):
        def run(after):
            name = f"fused_{side}"
            made = fused(halves_0[side], table=groups, carry=carry, name=name, after=(after,))
            own_pieces.append(made)
            return [made]

        return run

    windows = [own_beside(0, first_theirs), own_beside(1, first_mine)]
    whole = sum_wide(*following, windows, "wide_1")
    rest_pieces = [
        fused(which, table=others, carry=carry, name=f"fused_rest_{which.begin}")
        for which, carry in zip(rest, rest_prior)
    ]
    each = max(1, 8 // sizes.own)
    ahead = [[], []]
    arranged = []

    def ahead_beside(side):
        def run(after):
            for begin in range(0, wide_count // 2, each):
                ahead[side] += tiles(
                    Natural(side, begin, each * sizes.own),
                    block=1,
                    table=groups,
                    name=f"tiles_1_{side}_{begin}",
                    after=(after,),
                )
            made = list(ahead[side])
            if side:
                layout = [*halves_0, *halves_1, *rest]
                parts = [*own_pieces, *following, *rest_pieces]
                arranged.append(
                    arrange_part(sizes, layout, groups, others, update, parts, (after,))
                )
                made += arranged
            return made

        return run

    update_1 = weights(whole, 1, [ahead_beside(0), ahead_beside(1)])
    theirs, mine = (
        last_part(sizes, side, groups, update_1, arranged[0], ahead[side], f"last_{side}")
        for side in range(2)
    )
    return scatter_wide(theirs, mine), jnp.stack([update, update_1])


def solution(mesh):
    in_specs = (
        P(None, "narrow"),
        P(),
        P(None, "wide"),
        P("wide"),
        P(None, "wide"),
        P(("narrow", "wide")),
        P(None, ("narrow", "wide")),
        P(None, "wide", "narrow"),
        P(),
    )
    out_specs = (P(None, ("narrow", "wide")), P(None, None, "wide"))

    def run(points, scales, frequencies, *others):
        return jax.shard_map(
            functools.partial(on_device, frequencies.shape[1]),
            mesh=mesh,
            in_specs=in_specs,
            out_specs=out_specs,
            check_vma=False,
        )(points, scales, frequencies, *others)

    return run
```
